512 devices in a mesh: gz: 128 (over z, y, core), col: 4 (over x).
Axes of the slice: x: 4, y: 8, z: 8, core: 2. Of those that a mesh axis runs over, the one named last changes fastest.
Arguments:
- populations: bfloat16 [19, 256, 32, 512], P(None, 'gz', 'col'), may hold values from 0.5 to 1.5
- solid: int32 [256, 32, 512], P('gz', 'col'), may hold values 0 or 1
- radius: float32 [131072], P(('gz', 'col')), may hold values from 0.5 to 1.5
- rate: float32 [131072], P(('gz', 'col')), may hold values from 0.1 to 1
- ice_mass: float32 [131072], P(('gz', 'col')), may hold values from 1 to 3
- owner: int32 [131072, 1], P(('gz', 'col')), may hold values from 0 to 127; in each aligned block of 256 rows (0 to 255, 256 to 511, ...) at most 4 rows name the same one
- voxel: int32 [131072], P(('gz', 'col')), may hold values from 0 to 8191
Outputs:
- new_populations: bfloat16 [19, 256, 32, 512], P(None, 'gz', 'col')
- flux: float32 [131072], P(('gz', 'col'))
- ice_left: float32 [131072], P(('gz', 'col'))
The draws below stay inside these ranges and needn't reach their ends.
Inputs may be any that keep to these rules, and one draw needn't show every extreme that they name: Among the 256 records of one device at most 4 name the same owner, and some device reaches 4.
All inputs are finite; a program needn't handle non-finite values. No bound on the sum of `solid` on one device may be relied on, other than what follows from the above.
Results may differ from the reference program's by a relative error of at most 0.0041.
Values may be sent and summed in bfloat16 or wider, within the bound.
A program may use at most 64 MiB of HBM per device.

```python
import math
import jax
import jax.numpy as jnp
import numpy as np
from jax import lax

HZ = 2
CX = 8
Y = 512
DROP_DEV = 256
STEPS = 2
CAP = 4
NZ = 256
NX = 32
DROPS = 131072
N_GZ = 128
N_COL = 4


def plant(entries, own_key, smallest, high):
    longest = entries.shape.index(max(entries.shape))
    spots = []
    for shift in (0, 1):
        where = [jax.random.randint(jax.random.fold_in(own_key, axis), (), 0, length) for axis, length in enumerate(entries.shape)]
        where[longest] = (where[longest] + shift) % entries.shape[longest]
        spots.append(tuple(where))
    return entries.at[spots[0]].set(smallest).at[spots[1]].set(high)


def shard_levels(stream_key, shape, pieces, smallest, largest):
    loudness = 1.0
    for dim, parts in pieces:
        heights = jax.random.uniform(jax.random.fold_in(jax.random.fold_in(stream_key, 6), dim), (parts,), jnp.float32, smallest / len(pieces), largest / len(pieces))
        loudness = loudness * jnp.repeat(jnp.exp(heights), shape[dim] // parts).reshape((-1,) + (1,) * (len(shape) - 1 - dim))
    return loudness


def assign_block(own_key, own, number, rows, number_of, top, bound, skew):
    sequence = jax.random.permutation(own_key, number_of)
    packed, common = portions_of(number_of, rows * top, bound, skew, True), portions_of(number_of, rows * top, bound, skew, False)
    places = jnp.arange(number_of)

    def named(sizes, turn):
        used = int((sizes > 0).sum())
        fixed = max(1, used // 4)
        passed = fixed + (places - fixed + turn * (used - fixed)) % max(1, number_of - fixed)
        return jnp.zeros((number_of,), jnp.int32).at[sequence[jnp.where(places < fixed, places, passed)]].set(jnp.asarray(sizes, jnp.int32))

    sizes = jnp.where(number % 4 == 0, named(packed, number // 4), named(common, number - number // 4 - 1))
    mixed = jax.random.permutation(jax.random.fold_in(own, 3), number_of)
    giver, sink = mixed[0:number_of // 2 * 2:2], mixed[1:number_of // 2 * 2:2]
    slack = jnp.minimum(sizes[giver] - 1, bound - sizes[sink]) // 2
    slack = jnp.where((giver == sequence[0]) | (sink == sequence[0]) | (sizes[sink] == 0), 0, jnp.maximum(slack, 0))
    passed = jax.random.randint(jax.random.fold_in(own, 4), (number_of // 2,), 0, 1 << 20) % (slack + 1)
    sizes = sizes.at[giver].add(-passed).at[sink].add(passed)
    labels = jnp.searchsorted(jnp.cumsum(sizes), jnp.arange(rows * top), side="right").astype(jnp.int32)
    grid = labels.reshape(top, rows).T
    grid = grid[jax.random.permutation(jax.random.fold_in(own, 1), rows)]
    turn = jax.random.randint(jax.random.fold_in(own, 2), (rows, 1), 0, top)
    return jnp.take_along_axis(grid, (jnp.arange(top)[None, :] + turn) % top, axis=1)


def portions_of(count, total, bound, lean, full):
    loads = [(1 << 20) // math.isqrt(standing ** lean) + 1 for standing in range(1, count + 1)]
    largest = bound if full else min(bound, max(-(-total // count), total * loads[0] // sum(loads)))
    least = 1 if total - largest >= count - 1 else 0
    holding, rest = [largest] + [least] * (count - 1), total - largest - least * (count - 1)
    while rest > 0:
        candidates = [i for i in range(1, count) if holding[i] < largest] or [i for i in range(1, count) if holding[i] < bound]
        whole, remaining = sum([loads[i] for i in candidates]), rest
        for i in candidates:
            extra = min(bound - holding[i], max(1, remaining * loads[i] // whole), rest)
            holding[i] = holding[i] + extra
            rest = rest - extra
    return np.array(holding)


def setup_inputs(seed: int = 0) -> dict:
    streams_of = jax.random.split(jax.random.key(seed), 8)
    populations = jnp.clip(0.5 + 1.0 * jax.random.uniform(streams_of[0], (19, NZ, NX, Y), jnp.float32) ** shard_levels(streams_of[0], (19, NZ, NX, Y), ((1, 128), (2, 4)), -0.2, 0.2), 0.5, 1.5).astype(jnp.bfloat16)
    solid = plant((jax.random.randint(streams_of[1], (NZ, NX, Y), 0, 5) < 1).astype(jnp.int32), jax.random.fold_in(streams_of[1], 1), 0, 1)
    radius = jnp.clip(0.5 + 1.0 * jax.random.uniform(streams_of[2], (DROPS,), jnp.float32) ** shard_levels(streams_of[2], (DROPS,), ((0, 512),), -0.2, 0.2), 0.5, 1.5)
    rate = jnp.clip(jnp.exp(math.log(1.0) - 2.3025851 * jax.random.uniform(streams_of[3], (DROPS,), jnp.float32) ** shard_levels(streams_of[3], (DROPS,), ((0, 512),), -0.2, 0.2)), 0.1, 1.0)
    ice_mass = jnp.clip(1.0 + 2.0 * jax.random.uniform(streams_of[4], (DROPS,), jnp.float32) ** shard_levels(streams_of[4], (DROPS,), ((0, 512),), -0.2, 0.2), 1.0, 3.0)
    owner_keys = jax.random.split(jax.random.fold_in(streams_of[5], 1), DROPS // DROP_DEV)
    owner_turns = jax.random.permutation(jax.random.fold_in(streams_of[5], 3), DROPS // DROP_DEV)
    owner = jax.vmap(lambda own, number: assign_block(jax.random.fold_in(streams_of[5], 2), own, number, DROP_DEV, N_GZ, 1, CAP, 2))(owner_keys, owner_turns).reshape((DROPS, 1))
    voxel = plant(jax.random.randint(streams_of[6], (DROPS,), 0, HZ * CX * Y), jax.random.fold_in(streams_of[6], 1), 0, (HZ * CX * Y) - 1).astype(jnp.int32)
    return {"populations": populations, "solid": solid, "radius": radius, "rate": rate, "ice_mass": ice_mass, "owner": owner, "voxel": voxel}


VELOCITIES = [(0, 0, 0), (1, 0, 0), (-1, 0, 0), (0, 1, 0), (0, -1, 0), (0, 0, 1), (0, 0, -1),
              (1, 1, 0), (-1, -1, 0), (1, -1, 0), (-1, 1, 0), (1, 0, 1), (-1, 0, -1),
              (1, 0, -1), (-1, 0, 1), (0, 1, 1), (0, -1, -1), (0, 1, -1), (0, -1, 1)]
OPPOSITE = [0, 2, 1, 4, 3, 6, 5, 8, 7, 10, 9, 12, 11, 14, 13, 16, 15, 18, 17]
LATTICE_WEIGHTS = [1.0 / 3.0] + [1.0 / 18.0] * 6 + [1.0 / 36.0] * 12
OMEGA = 1.6


def moment_table():
    rows = [LATTICE_WEIGHTS]
    for axis_pos in range(3):
        rows.append([LATTICE_WEIGHTS[q] * VELOCITIES[q][axis_pos] for q in range(19)])
    return jnp.array(rows, jnp.float32)


def moments(values):
    return jnp.tensordot(moment_table(), values, axes=1, precision=lax.Precision.HIGHEST)


def collide(pops, solid_flag, source):
    values = pops.astype(jnp.float32)
    stats = moments(values)
    density = stats[0]
    velocity = stats[1:] / density
    along = jnp.tensordot(jnp.array(VELOCITIES, jnp.float32), velocity, axes=1, precision=lax.Precision.HIGHEST)
    square = jnp.sum(velocity * velocity, 0)
    balance = density * (1.0 + 3.0 * along + 4.5 * along * along - 1.5 * square)
    relaxed = values - OMEGA * (values - balance) + source.astype(jnp.float32)
    bounced = jnp.stack([values[k] for k in OPPOSITE])
    return jnp.where(solid_flag, bounced, relaxed).astype(jnp.bfloat16)


def stream(padded):
    depth = padded.shape[1] - 2
    across = padded.shape[2] - 2
    moved = []
    for q in range(19):
        cz, cx, cy = VELOCITIES[q]
        piece = padded[q, 1 - cz:1 - cz + depth, 1 - cx:1 - cx + across, :]
        moved.append(jnp.roll(piece, cy, axis=2))
    return jnp.stack(moved)


def reference(populations, solid, radius, rate, ice_mass, owner, voxel):
    density0 = moments(populations.astype(jnp.float32))[0]
    count = radius.shape[0]
    index = jnp.arange(count, dtype=jnp.int32)
    column = (index // DROP_DEV) % N_COL
    target = owner[:, 0]
    zpos = target * HZ + voxel // (CX * Y)
    xpos = column * CX + (voxel // Y) % CX
    ypos = voxel % Y
    coef = rate * radius * radius
    flux = coef * (2.0 - density0[zpos, xpos, ypos])
    ice_left = ice_mass - flux
    source = jnp.zeros(density0.shape, jnp.float32).at[zpos, xpos, ypos].add(0.5 * flux).astype(jnp.bfloat16)
    solid_flag = solid > 0
    state = populations
    for step in range(STEPS):
        post = collide(state, solid_flag, source)
        padded = jnp.pad(post, ((0, 0), (1, 1), (1, 1), (0, 0)))
        state = stream(padded)
    return state, flux, ice_left
```

```python
import jax
import jax.numpy as jnp
from jax import lax
from jax.experimental import pallas as pl
from jax.experimental.pallas import tpu as pltpu
from jax.sharding import PartitionSpec as P

STEPS = 2
MESH = pl.DeviceIdType.MESH
HIGHEST = lax.Precision.HIGHEST
f32 = jnp.float32
bf16 = jnp.bfloat16


def hops(pair):
    o, e = pair
    return min(o, 8 - o) + min(e, 16 - e) / 2


PEERS = sorted([(o, e) for o in range(8) for e in range(16) if (o, e) != (0, 0)], key=lambda p: -hops(p))


def peer(z, d, o, e):
    return lax.rem(z + o, 8) * 16 + lax.rem(d + e, 16)


def greet_group(sem, z, d):
    for o, e in PEERS:
        pl.semaphore_signal(sem, inc=1, device_id={"gz": peer(z, d, o, e)}, device_id_type=MESH)


def send_rows(src, dst, send, recv, z, d, sign):
    for o, e in PEERS:
        row = pl.ds(o * 16 + e, 1)
        to = peer(z, d, o, e) if sign > 0 else peer(z, d, (8 - o) % 8, (16 - e) % 16)
        pltpu.make_async_remote_copy(
            src_ref=src.at[row],
            dst_ref=dst.at[row],
            send_sem=send,
            recv_sem=recv,
            device_id={"gz": to},
            device_id_type=MESH,
        ).start()


def wait_rows(buf, sem):
    rows = buf.at[pl.ds(1, 127)]
    pltpu.make_async_copy(rows, rows, sem).wait()


def iota(shape, dim):
    return lax.broadcasted_iota(jnp.int32, shape, dim)


def flat_row(ref):
    return jnp.concatenate([ref[0:1, :], ref[1:2, :]], axis=1)


def dot_t(a, b):
    return lax.dot_general(a, b, (((1,), (1,)), ((), ())), precision=HIGHEST, preferred_element_type=f32)


def dot(a, b):
    return jnp.dot(a, b, precision=HIGHEST, preferred_element_type=f32)


def request_table(own_ref, vox_ref, rad_ref, rate_ref, z, d):
    own, vox = flat_row(own_ref), flat_row(vox_ref)
    rad, rate = flat_row(rad_ref), flat_row(rate_ref)
    coef = rate * rad * rad
    rel = (((own >> 4) - z) & 7) * 16 + (((own & 15) - d) & 15)
    named = (iota((128, 256), 0) == rel).astype(f32)
    earlier = (iota((256, 256), 0) < iota((256, 256), 1)).astype(bf16)
    before = jnp.dot(named.astype(bf16), earlier, preferred_element_type=f32)
    rank = jnp.sum(before * named, axis=0, keepdims=True).astype(jnp.int32)
    lane = iota((128, 256), 0)
    value = jnp.where(lane < 4, coef, jnp.where(lane < 8, vox.astype(f32), 0.0))
    value = jnp.where((lane & 3) == rank, value, 0.0)
    return dot_t(named, value), named, rank, coef


def serve(table, density):
    rows = jnp.transpose(table)
    coef = jnp.concatenate([rows[k : k + 1, :] for k in range(4)], axis=1)
    code = jnp.concatenate([rows[k : k + 1, :] for k in range(4, 8)], axis=1).astype(jnp.int32)
    hi = ((code >> 7) & 3) * 16 + (code >> 9)
    lo = code & 127
    at_hi = (iota((128, 512), 0) == hi).astype(f32)
    at_lo = iota((128, 512), 0) == lo
    field = jnp.concatenate([density[:, c * 128 : (c + 1) * 128] for c in range(4)] + [jnp.zeros((64, 128), f32)], axis=0)
    picked = dot(jnp.transpose(field), at_hi)
    rho = jnp.sum(jnp.where(at_lo, picked, 0.0), axis=0, keepdims=True)
    answer = 2.0 - rho
    spread = jnp.where(at_lo, 0.5 * coef * answer, 0.0)
    total = dot_t(at_hi, spread)
    source = jnp.concatenate([total[c * 16 : (c + 1) * 16, :] for c in range(4)], axis=1)
    reply = jnp.concatenate([answer[:, k * 128 : (k + 1) * 128] for k in range(4)] + [jnp.zeros((124, 128), f32)], axis=0)
    return jnp.transpose(reply), source


def read_reply(reply, named, rank, coef):
    rows = jnp.transpose(reply)[0:8, :]
    got = dot(rows, named)
    answer = jnp.sum(jnp.where(iota((8, 256), 0) == rank, got, 0.0), axis=0, keepdims=True)
    return coef * answer


VELOCITIES = [
    (0, 0, 0),
    (1, 0, 0),
    (-1, 0, 0),
    (0, 1, 0),
    (0, -1, 0),
    (0, 0, 1),
    (0, 0, -1),
    (1, 1, 0),
    (-1, -1, 0),
    (1, -1, 0),
    (-1, 1, 0),
    (1, 0, 1),
    (-1, 0, -1),
    (1, 0, -1),
    (-1, 0, 1),
    (0, 1, 1),
    (0, -1, -1),
    (0, 1, -1),
    (0, -1, 1),
]
OPPOSITE = [0, 2, 1, 4, 3, 6, 5, 8, 7, 10, 9, 12, 11, 14, 13, 16, 15, 18, 17]
LATTICE_WEIGHTS = [1.0 / 3.0] + [1.0 / 18.0] * 6 + [1.0 / 36.0] * 12
OMEGA = 1.6


def density_of(pops):
    near = pops[1]
    for q in range(2, 7):
        near = near + pops[q]
    far = pops[7]
    for q in range(8, 19):
        far = far + pops[q]
    return pops[0] * (1.0 / 3.0) + near * (1.0 / 18.0) + far * (1.0 / 36.0)


def droplets(own, vox, rad, rate, pops, flux, source, ask, asked, tell, told, sends, recvs):
    me = lax.axis_index("gz")
    z, d = me // 16, lax.rem(me, 16)
    barrier = pltpu.get_barrier_semaphore()
    greet_group(barrier, z, d)
    table, named, rank, coef = request_table(own, vox, rad, rate, z, d)
    ask[...] = table
    density = density_of([pops[q].astype(f32) for q in range(19)])
    pl.semaphore_wait(barrier, 127)
    send_rows(ask, asked, sends.at[0], recvs.at[0], z, d, 1)
    asked[0:1, :] = ask[0:1, :]
    wait_rows(asked, recvs.at[0])
    reply, total = serve(asked[...], density)
    tell[...] = reply
    send_rows(tell, told, sends.at[1], recvs.at[1], z, d, -1)
    told[0:1, :] = tell[0:1, :]
    source[...] = total
    wait_rows(told, recvs.at[1])
    row = read_reply(told[...], named, rank, coef)
    flux[0:1, :] = row[:, 0:128]
    flux[1:2, :] = row[:, 128:256]
    wait_rows(ask, sends.at[0])
    wait_rows(tell, sends.at[1])


def extended(array, sides, width):
    for axis, dim in sides:
        size, length = (lax.axis_size(axis), array.shape[dim])
        up = [(i, (i + 1) % size) for i in range(size - 1)]
        down = [(j, i) for i, j in up]
        last = lax.slice_in_dim(array, length - width, length, axis=dim)
        leading = lax.slice_in_dim(array, 0, width, axis=dim)
        before = lax.ppermute(last, axis, up)
        after = lax.ppermute(leading, axis, down)
        array = jnp.concatenate([before, array, after], axis=dim)
    return array


def moment_table():
    rows = [LATTICE_WEIGHTS]
    for axis_pos in range(3):
        rows.append([LATTICE_WEIGHTS[q] * VELOCITIES[q][axis_pos] for q in range(19)])
    return jnp.array(rows, jnp.float32)


def moments(values):
    return jnp.tensordot(moment_table(), values, axes=1, precision=lax.Precision.HIGHEST)


def collide(pops, solid_flag, source):
    values = pops.astype(jnp.float32)
    stats = moments(values)
    density = stats[0]
    velocity = stats[1:] / density
    along = jnp.tensordot(
        jnp.array(VELOCITIES, jnp.float32), velocity, axes=1, precision=lax.Precision.HIGHEST
    )
    square = jnp.sum(velocity * velocity, 0)
    balance = density * (1.0 + 3.0 * along + 4.5 * along * along - 1.5 * square)
    relaxed = values - OMEGA * (values - balance) + source.astype(jnp.float32)
    bounced = jnp.stack([values[k] for k in OPPOSITE])
    result = jnp.where(solid_flag, bounced, relaxed)
    return result.astype(jnp.bfloat16)


def stream(padded):
    depth = padded.shape[1] - 2
    across = padded.shape[2] - 2
    moved = []
    for q in range(19):
        cz, cx, cy = VELOCITIES[q]
        piece = padded[q, 1 - cz : 1 - cz + depth, 1 - cx : 1 - cx + across, :]
        moved.append(jnp.roll(piece, cy, axis=2))
    return jnp.stack(moved)


def body(populations, solid, radius, rate, ice_mass, owner, voxel):
    pops = populations.reshape(19, 16, 512)
    vm = pl.BlockSpec(memory_space=pltpu.VMEM)
    flux, source = pl.pallas_call(
        droplets,
        out_shape=(jax.ShapeDtypeStruct((2, 128), f32), jax.ShapeDtypeStruct((16, 512), f32)),
        in_specs=[vm] * 5,
        out_specs=(vm, vm),
        scratch_shapes=[pltpu.VMEM((128, 128), f32)] * 4 + [pltpu.SemaphoreType.DMA((2,))] * 2,
        name="droplets",
        compiler_params=pltpu.CompilerParams(collective_id=0, has_side_effects=True, vmem_limit_bytes=32 * 2**20),
    )(owner.reshape(2, 128), voxel.reshape(2, 128), radius.reshape(2, 128), rate.reshape(2, 128), pops)
    flux = flux.reshape(-1)
    source = source.reshape(solid.shape).astype(bf16)
    solid_flag = solid > 0
    state = populations
    for step in range(STEPS):
        post = collide(state, solid_flag, source)
        padded = extended(post, (("gz", 1), ("col", 2)), 1)
        state = stream(padded)
    return (state, flux, ice_mass - flux)


def solution(mesh):
    return jax.shard_map(
        body,
        mesh=mesh,
        in_specs=(
            P(None, "gz", "col", None),
            P("gz", "col", None),
            P(("gz", "col")),
            P(("gz", "col")),
            P(("gz", "col")),
            P(("gz", "col"), None),
            P(("gz", "col")),
        ),
        out_specs=(P(None, "gz", "col", None), P(("gz", "col")), P(("gz", "col"))),
        check_vma=False,
    )
```

```python
import jax
import jax.numpy as jnp
from jax import lax
from jax.experimental import pallas as pl
from jax.experimental.pallas import tpu as pltpu
from jax.sharding import PartitionSpec as P

MESH = pl.DeviceIdType.MESH
HIGHEST = lax.Precision.HIGHEST
f32 = jnp.float32
bf16 = jnp.bfloat16


def hops(pair):
    o, e = pair
    return min(o, 8 - o) + min(e, 16 - e) / 2


PEERS = sorted([(o, e) for o in range(8) for e in range(16) if (o, e) != (0, 0)], key=lambda p: -hops(p))


def peer(z, d, o, e):
    return lax.rem(z + o, 8) * 16 + lax.rem(d + e, 16)


def greet_group(sem, z, d):
    for o, e in PEERS:
        pl.semaphore_signal(sem, inc=1, device_id={"gz": peer(z, d, o, e)}, device_id_type=MESH)


def send_rows(src, dst, send, recv, z, d, sign):
    for o, e in PEERS:
        row = pl.ds(o * 16 + e, 1)
        to = peer(z, d, o, e) if sign > 0 else peer(z, d, (8 - o) % 8, (16 - e) % 16)
        pltpu.make_async_remote_copy(
            src_ref=src.at[row],
            dst_ref=dst.at[row],
            send_sem=send,
            recv_sem=recv,
            device_id={"gz": to},
            device_id_type=MESH,
        ).start()


def wait_rows(buf, sem):
    rows = buf.at[pl.ds(1, 127)]
    pltpu.make_async_copy(rows, rows, sem).wait()


def iota(shape, dim):
    return lax.broadcasted_iota(jnp.int32, shape, dim)


def flat_row(ref):
    return jnp.concatenate([ref[0:1, :], ref[1:2, :]], axis=1)


def dot_t(a, b):
    return lax.dot_general(a, b, (((1,), (1,)), ((), ())), precision=HIGHEST, preferred_element_type=f32)


def dot(a, b):
    return jnp.dot(a, b, precision=HIGHEST, preferred_element_type=f32)


def request_table(own_ref, vox_ref, rad_ref, rate_ref, z, d):
    own, vox = flat_row(own_ref), flat_row(vox_ref)
    rad, rate = flat_row(rad_ref), flat_row(rate_ref)
    coef = rate * rad * rad
    rel = (((own >> 4) - z) & 7) * 16 + (((own & 15) - d) & 15)
    named = (iota((128, 256), 0) == rel).astype(f32)
    earlier = (iota((256, 256), 0) < iota((256, 256), 1)).astype(bf16)
    before = jnp.dot(named.astype(bf16), earlier, preferred_element_type=f32)
    rank = jnp.sum(before * named, axis=0, keepdims=True).astype(jnp.int32)
    lane = iota((128, 256), 0)
    value = jnp.where(lane < 4, coef, jnp.where(lane < 8, vox.astype(f32), 0.0))
    value = jnp.where((lane & 3) == rank, value, 0.0)
    return dot_t(named, value), named, rank, coef


def serve(table, density):
    rows = jnp.transpose(table)
    coef = jnp.concatenate([rows[k : k + 1, :] for k in range(4)], axis=1)
    code = jnp.concatenate([rows[k : k + 1, :] for k in range(4, 8)], axis=1).astype(jnp.int32)
    hi = ((code >> 7) & 3) * 16 + (code >> 9)
    lo = code & 127
    at_hi = (iota((128, 512), 0) == hi).astype(f32)
    at_lo = iota((128, 512), 0) == lo
    field = jnp.concatenate([density[:, c * 128 : (c + 1) * 128] for c in range(4)] + [jnp.zeros((64, 128), f32)], axis=0)
    picked = dot(jnp.transpose(field), at_hi)
    rho = jnp.sum(jnp.where(at_lo, picked, 0.0), axis=0, keepdims=True)
    answer = 2.0 - rho
    spread = jnp.where(at_lo, 0.5 * coef * answer, 0.0)
    total = dot_t(at_hi, spread)
    source = jnp.concatenate([total[c * 16 : (c + 1) * 16, :] for c in range(4)], axis=1)
    reply = jnp.concatenate([answer[:, k * 128 : (k + 1) * 128] for k in range(4)] + [jnp.zeros((124, 128), f32)], axis=0)
    return jnp.transpose(reply), source


def read_reply(reply, named, rank):
    rows = jnp.transpose(reply)[0:8, :]
    got = dot(rows, named)
    return jnp.sum(jnp.where(iota((8, 256), 0) == rank, got, 0.0), axis=0, keepdims=True)


VELOCITIES = [
    (0, 0, 0),
    (1, 0, 0),
    (-1, 0, 0),
    (0, 1, 0),
    (0, -1, 0),
    (0, 0, 1),
    (0, 0, -1),
    (1, 1, 0),
    (-1, -1, 0),
    (1, -1, 0),
    (-1, 1, 0),
    (1, 0, 1),
    (-1, 0, -1),
    (1, 0, -1),
    (-1, 0, 1),
    (0, 1, 1),
    (0, -1, -1),
    (0, 1, -1),
    (0, -1, 1),
    (0, 0, 0),
]
FLAG = 19
UP = [q for q in range(19) if VELOCITIES[q][0] == 1]
FLAT = [q for q in range(20) if VELOCITIES[q][0] == 0]
DOWN = [q for q in range(19) if VELOCITIES[q][0] == -1]
ZPLACE = {q: i for i, q in enumerate(UP + FLAT + DOWN)}
XUP = [q for q in range(19) if VELOCITIES[q][1] == 1]
XFLAT = [q for q in range(20) if VELOCITIES[q][1] == 0]
XDOWN = [q for q in range(19) if VELOCITIES[q][1] == -1]
XTILES = XUP + XUP[-1:] + XFLAT + XDOWN + XDOWN[-1:]
XPLACE = {q: XTILES.index(q) for q in range(20)}
NEAR = [(a, b) for a in (-1, 0, 1) for b in (-1, 0, 1) if (a, b) != (0, 0)]
ASIDE = [(a, b) for a, b in NEAR if b != 0]


def dotc(c, v):
    total = None
    for k, x in zip(c, v):
        if k:
            total = (x if k > 0 else -x) if total is None else (total + x if k > 0 else total - x)
    return total


def total_of(terms):
    out = terms[0]
    for t in terms[1:]:
        out = out + t
    return out


def density_of(g):
    near = total_of([g[q] for q in range(1, 7)])
    far = total_of([g[q] for q in range(7, 19)])
    return g[0] * (1.0 / 3.0) + near * (1.0 / 18.0) + far * (1.0 / 36.0)


def collide(g, solid, source, wanted):
    diff = {q: g[q] - g[q + 1] for q in range(1, 19, 2)}
    rho = density_of(g)
    j = []
    for axis in range(3):
        far = None
        for q in range(7, 19, 2):
            k = VELOCITIES[q][axis]
            if k:
                far = diff[q] if far is None else (far + diff[q] if k > 0 else far - diff[q])
        j.append(diff[1 + 2 * axis] * (4.8 / 18.0) + far * (4.8 / 36.0))
    scale = (1.5 / 4.8) / rho
    u = [x * scale for x in j]
    own = [x * y for x, y in zip(j, u)]
    base = 1.6 * rho - (own[0] + own[1] + own[2]) * (1.0 / 3.0)
    if source is not None:
        base = base + source
    out = {}
    if 0 in wanted:
        out[0] = jnp.where(solid, g[0], base - 0.6 * g[0])
    for q in range(1, 19, 2):
        if q not in wanted and q + 1 not in wanted:
            continue
        odd = dotc(VELOCITIES[q], j)
        even = base + (own[q // 2] if q < 7 else odd * dotc(VELOCITIES[q], u))
        if q in wanted:
            out[q] = jnp.where(solid, g[q + 1], even + odd - 0.6 * g[q])
        if q + 1 in wanted:
            out[q + 1] = jnp.where(solid, g[q], even - odd - 0.6 * g[q + 1])
    return out, rho


def wide(ref, q, rows):
    return jnp.concatenate([ref[q, c, rows, :] for c in range(4)], axis=1)


def put(ref, q, rows, value):
    for c in range(4):
        ref[q, c, rows, :] = value[:, 128 * c : 128 * c + 128]


def lane_roll(x, cy):
    return x if cy == 0 else pltpu.roll(x, cy % 512, 1)


def row_roll(x, k):
    return pltpu.roll(x, k % x.shape[0], 0)


def remote(src, dst, send, recv, gz, col):
    return pltpu.make_async_remote_copy(
        src_ref=src, dst_ref=dst, send_sem=send, recv_sem=recv, device_id={"gz": gz, "col": col}, device_id_type=MESH
    )


def step_pair(own, vox, rad, rate, solid, pops, out, answer, *scratch):
    (own_v, vox_v, rad_v, rate_v, solid_v, pops_v, ask, asked, tell, told, rel, below, above, edge, left, right) = scratch[:16]
    (src, near, spread, work, post, dens, loads, sends, recvs, zsend, zrecv, xsend, xrecv, nsend, nrecv) = scratch[16:]
    gz, col = lax.axis_index("gz"), lax.axis_index("col")
    z, d = gz // 16, lax.rem(gz, 16)
    barrier = pltpu.get_barrier_semaphore()

    fetch = [
        pltpu.make_async_copy(a, b, loads.at[i])
        for i, (a, b) in enumerate(
            [(own, own_v), (vox, vox_v), (rad, rad_v), (rate, rate_v), (solid, solid_v), (pops, pops_v)]
        )
    ]
    for c in fetch:
        c.start()
    greet_group(barrier, z, d)

    def beside(dz, dx):
        return lax.rem(gz + dz + 128, 128), lax.rem(col + dx + 4, 4)

    for dz, dx in ASIDE:
        g, c = beside(dz, dx)
        pl.semaphore_signal(barrier, inc=1, device_id={"gz": g, "col": c}, device_id_type=MESH)
    for c in fetch:
        c.wait()
    table, named, rank, coef = request_table(own_v, vox_v, rad_v, rate_v, z, d)
    ask[...] = table

    def first(i, carry):
        lanes = pl.ds(pl.multiple_of(i * 128, 128), 128)
        g = [pops_v[q, :, lanes].astype(f32) for q in range(19)]
        made, rho = collide(g, solid_v[:, lanes] > 0, None, range(19))
        dens[:, lanes] = rho
        for q in range(19):
            post[q, i, 0:16, :] = made[q]
        return carry

    lax.fori_loop(0, 4, first, 0)
    for q in range(19):
        rel[ZPLACE[q]] = lane_roll(wide(post, q, pl.ds(0, 16)), VELOCITIES[q][2]).astype(bf16)
    rel[ZPLACE[FLAG]] = jnp.where(solid_v[...] > 0, 1.0, 0.0).astype(bf16)

    pl.semaphore_wait(barrier, 127 + len(ASIDE))
    up, down = beside(1, 0), beside(-1, 0)
    zcopies = [
        remote(rel.at[pl.ds(0, 15)], below, zsend.at[0], zrecv.at[0], *up),
        remote(rel.at[pl.ds(5, 15)], above, zsend.at[1], zrecv.at[1], *down),
    ]
    for c in zcopies:
        c.start()
    send_rows(ask, asked, sends.at[0], recvs.at[0], z, d, 1)
    asked[0:1, :] = ask[0:1, :]

    for c in zcopies:
        c.wait_recv()
    has_below, has_above = gz > 0, gz < 127
    for q in range(20):
        cz, i = VELOCITIES[q][0], ZPLACE[q]
        mine = rel[i].astype(f32)
        if cz >= 0:
            under = jnp.where(has_below, below[i].astype(f32), 0.0)
        if cz <= 0:
            over = jnp.where(has_above, above[i - 5].astype(f32), 0.0)
        if cz == 1:
            rows = [under, mine]
        elif cz == -1:
            rows = [mine, over]
        else:
            rows = [under[8:16], mine, over[0:8]]
        put(work, q, pl.ds(0, 32), jnp.concatenate(rows, axis=0))

    def column(q, x):
        return wide(work, q, pl.ds(x, 4, stride=8))

    def edge_tile(q):
        cx = VELOCITIES[q][1]
        first_x, then_x = {0: (7, 0), 1: (7, 6), -1: (0, 1)}[cx]
        return jnp.concatenate([column(q, first_x), column(q, then_x)], axis=0)

    for b in range(11):
        edge[b] = jnp.concatenate([edge_tile(XTILES[2 * b]), edge_tile(XTILES[2 * b + 1])], axis=0).astype(bf16)
    to_right, to_left = beside(0, 1), beside(0, -1)
    xcopies = [
        remote(edge.at[pl.ds(0, 8)], left, xsend.at[0], xrecv.at[0], *to_right),
        remote(edge.at[pl.ds(3, 8)], right, xsend.at[1], xrecv.at[1], *to_left),
    ]
    for c in xcopies:
        c.start()

    wait_rows(asked, recvs.at[0])
    reply, total = serve(asked[...], dens[...])
    src[...] = jnp.where(solid_v[...] > 0, 0.0, total).astype(bf16)
    ncopies = []
    for i, (dz, dx) in enumerate(NEAR):
        ncopies.append(remote(src, near.at[7 - i], nsend.at[i], nrecv.at[7 - i], *beside(dz, dx)))
    for c in ncopies:
        c.start()
    tell[...] = reply
    send_rows(tell, told, sends.at[1], recvs.at[1], z, d, -1)
    told[0:1, :] = tell[0:1, :]

    for c in xcopies:
        c.wait_recv()
    has_left, has_right = col > 0, col < 3
    row8 = iota((8, 512), 0)

    def tile(ref, shift, q, there):
        k = XPLACE[q] - shift
        both = jnp.where(there, ref[k // 2].astype(f32), 0.0)
        return both[8 * (k % 2) : 8 * (k % 2) + 8]

    for q in range(20):
        cx = VELOCITIES[q][1]
        if cx == 0:
            put(work, q, pl.ds(32, 8), jnp.where(row8 < 4, tile(left, 0, q, has_left), tile(right, 6, q, has_right)))
        else:
            ends = tile(left, 0, q, has_left) if cx == 1 else tile(right, 6, q, has_right)
            k = XPLACE[q]
            mine = edge[k // 2].astype(f32)[8 * (k % 2) : 8 * (k % 2) + 8]
            merged = jnp.where(row8 < 4, mine, ends)
            put(work, q, pl.ds(32, 8), row_roll(merged, 4) if cx == 1 else merged)
            put(work, q, pl.ds(0, 32), row_roll(wide(work, q, pl.ds(0, 32)), cx))
            put(work, q, pl.ds(0 if cx == 1 else 7, 4, stride=8), ends[0:4])

    for i in range(8):
        remote(src, near.at[i], nsend.at[7 - i], nrecv.at[i], gz, col).wait_recv()
    for a in (-1, 0, 1):
        for b in (-1, 0, 1):
            there = True
            if (a, b) == (0, 0):
                block = src[...].astype(f32)
            else:
                block = near[NEAR.index((a, b))].astype(f32)
                if a:
                    there = has_below if a < 0 else has_above
                if b:
                    sideways = has_left if b < 0 else has_right
                    there = jnp.logical_and(there, sideways) if a else sideways
                block = jnp.where(there, block, 0.0)
            for k in (0, 1):
                plane = block[8 * k : 8 * k + 8]
                at = 16 * (2 * (a + 1) + k)
                for cy in (-1, 0, 1):
                    moved = lane_roll(plane, cy)
                    if b == 0:
                        put(spread, cy + 1, pl.ds(at + 2, 8), moved)
                    elif b < 0:
                        put(spread, cy + 1, pl.ds(at, 2), moved[6:8])
                    else:
                        put(spread, cy + 1, pl.ds(at + 10, 2), moved[0:2])
    for q in range(20):
        cz, cx, cy = VELOCITIES[q]
        rows = [pl.ds(16 * (p + 1 - cz) + 2 - cx, 8) for p in range(4)]
        rows += [pl.ds(16 * (1 - cz) + k - cx, 4, stride=16) for k in (1, 10)]
        for c in range(4):
            added = jnp.concatenate([spread[cy + 1, c, r, :] for r in rows], axis=0)
            if q == FLAG:
                post[FLAG, c] = added
            else:
                work[q, c] = (work[q, c] + added).astype(bf16).astype(f32)

    row = iota((8, 128), 0)
    plane_in = jnp.logical_and(
        jnp.logical_or((row & 3) != 0, has_below), jnp.logical_or((row & 3) != 3, has_above)
    )
    side_in = jnp.logical_or(jnp.logical_and(row < 4, has_left), jnp.logical_and(row >= 4, has_right))
    edge_in = jnp.logical_and(plane_in, side_in)
    jobs = [(8, range(19), None), (16, range(19), None), (0, UP, has_below), (24, DOWN, has_above), (32, XUP + XDOWN, edge_in)]

    def second(i, carry):
        for r, wanted, inside in jobs:
            rows = pl.ds(r, 8)
            g = [work[q, i, rows, :] for q in range(19)]
            made, _ = collide(g, work[FLAG, i, rows, :] > 0.5, post[FLAG, i, rows, :], wanted)
            for q in wanted:
                post[q, i, rows, :] = made[q] if inside is None else jnp.where(inside, made[q], 0.0)
        return carry

    lax.fori_loop(0, 4, second, 0)
    for q in range(19):
        cz, cx, cy = VELOCITIES[q]
        r = 8 * (1 - cz)
        moved = wide(post, q, pl.ds(r, 16))
        if cx:
            moved = row_roll(moved, cx)
            rim = 32 + (1 - cz) if cx == 1 else 36 + (1 - cz)
            for k in (0, 1):
                at = 8 * k + (0 if cx == 1 else 7)
                moved = jnp.where(iota((16, 512), 0) == at, wide(post, q, pl.ds(rim + k, 1)), moved)
        out[q] = lane_roll(moved, cy).astype(bf16)

    wait_rows(told, recvs.at[1])
    line = read_reply(told[...], named, rank)
    answer[0:1, :] = line[:, 0:128]
    answer[1:2, :] = line[:, 128:256]
    wait_rows(ask, sends.at[0])
    wait_rows(tell, sends.at[1])
    for c in zcopies + xcopies + ncopies:
        c.wait_send()


def body(populations, solid, radius, rate, ice_mass, owner, voxel):
    vm = pl.BlockSpec(memory_space=pltpu.VMEM)
    anywhere = pl.BlockSpec(memory_space=pl.ANY)
    sem = pltpu.SemaphoreType.DMA
    small = [pltpu.VMEM((2, 128), jnp.int32)] * 2 + [pltpu.VMEM((2, 128), f32)] * 2
    state, answer = pl.pallas_call(
        step_pair,
        out_shape=(jax.ShapeDtypeStruct((19, 16, 512), bf16), jax.ShapeDtypeStruct((2, 128), f32)),
        in_specs=[anywhere] * 6,
        out_specs=(vm, vm),
        scratch_shapes=small
        + [pltpu.VMEM((16, 512), jnp.int32), pltpu.VMEM((19, 16, 512), bf16)]
        + [pltpu.VMEM((128, 128), f32)] * 4
        + [pltpu.VMEM((20, 16, 512), bf16)]
        + [pltpu.VMEM((15, 16, 512), bf16)] * 2
        + [pltpu.VMEM((11, 16, 512), bf16)]
        + [pltpu.VMEM((8, 16, 512), bf16)] * 2
        + [pltpu.VMEM((16, 512), bf16), pltpu.VMEM((8, 16, 512), bf16)]
        + [pltpu.VMEM((3, 4, 96, 128), f32)]
        + [pltpu.VMEM((20, 4, 40, 128), f32)] * 2
        + [pltpu.VMEM((16, 512), f32)]
        + [sem((6,))]
        + [sem((2,))] * 6
        + [sem((8,))] * 2,
        name="two_steps",
        compiler_params=pltpu.CompilerParams(collective_id=0, has_side_effects=True, vmem_limit_bytes=48 * 2**20),
    )(
        owner.reshape(2, 128),
        voxel.reshape(2, 128),
        radius.reshape(2, 128),
        rate.reshape(2, 128),
        solid.reshape(16, 512),
        populations.reshape(19, 16, 512),
    )
    flux = rate * radius * radius * answer.reshape(-1)
    return (state.reshape(populations.shape), flux, ice_mass - flux)


def solution(mesh):
    return jax.shard_map(
        body,
        mesh=mesh,
        in_specs=(
            P(None, "gz", "col", None),
            P("gz", "col", None),
            P(("gz", "col")),
            P(("gz", "col")),
            P(("gz", "col")),
            P(("gz", "col"), None),
            P(("gz", "col")),
        ),
        out_specs=(P(None, "gz", "col", None), P(("gz", "col")), P(("gz", "col"))),
        check_vma=False,
    )
```

```python
import jax
import jax.numpy as jnp
from jax import lax
from jax.experimental import pallas as pl
from jax.experimental.pallas import tpu as pltpu
from jax.sharding import PartitionSpec as P

MESH = pl.DeviceIdType.MESH
HIGHEST = lax.Precision.HIGHEST
f32 = jnp.float32
bf16 = jnp.bfloat16


def hops(pair):
    o, e = pair
    return min(o, 8 - o) + min(e, 16 - e) / 2


PEERS = sorted([(o, e) for o in range(8) for e in range(16) if (o, e) != (0, 0)], key=lambda p: -hops(p))


def peer(z, d, o, e):
    return lax.rem(z + o, 8) * 16 + lax.rem(d + e, 16)


def greet_group(sem, z, d):
    for o, e in PEERS:
        pl.semaphore_signal(sem, inc=1, device_id={"gz": peer(z, d, o, e)}, device_id_type=MESH)


def send_rows(src, dst, send, recv, z, d, sign):
    for o, e in PEERS:
        row = pl.ds(o * 16 + e, 1)
        to = peer(z, d, o, e) if sign > 0 else peer(z, d, (8 - o) % 8, (16 - e) % 16)
        pltpu.make_async_remote_copy(
            src_ref=src.at[row],
            dst_ref=dst.at[row],
            send_sem=send,
            recv_sem=recv,
            device_id={"gz": to},
            device_id_type=MESH,
        ).start()


def wait_rows(buf, sem):
    rows = buf.at[pl.ds(1, 127)]
    pltpu.make_async_copy(rows, rows, sem).wait()


def iota(shape, dim):
    return lax.broadcasted_iota(jnp.int32, shape, dim)


def flat_row(ref):
    return jnp.concatenate([ref[0:1, :], ref[1:2, :]], axis=1)


def dot_t(a, b):
    return lax.dot_general(a, b, (((1,), (1,)), ((), ())), precision=HIGHEST, preferred_element_type=f32)


def dot(a, b):
    return jnp.dot(a, b, precision=HIGHEST, preferred_element_type=f32)


def request_table(own_ref, vox_ref, rad_ref, rate_ref, z, d):
    own, vox = flat_row(own_ref), flat_row(vox_ref)
    rad, rate = flat_row(rad_ref), flat_row(rate_ref)
    coef = rate * rad * rad
    rel = (((own >> 4) - z) & 7) * 16 + (((own & 15) - d) & 15)
    named = (iota((128, 256), 0) == rel).astype(f32)
    earlier = (iota((256, 256), 0) < iota((256, 256), 1)).astype(bf16)
    before = jnp.dot(named.astype(bf16), earlier, preferred_element_type=f32)
    rank = jnp.sum(before * named, axis=0, keepdims=True).astype(jnp.int32)
    lane = iota((128, 256), 0)
    value = jnp.where(lane < 4, coef, jnp.where(lane < 8, vox.astype(f32), 0.0))
    value = jnp.where((lane & 3) == rank, value, 0.0)
    return dot_t(named, value), named, rank, coef


def serve(table, density):
    rows = jnp.transpose(table)
    coef = jnp.concatenate([rows[k : k + 1, :] for k in range(4)], axis=1)
    code = jnp.concatenate([rows[k : k + 1, :] for k in range(4, 8)], axis=1).astype(jnp.int32)
    hi = ((code >> 7) & 3) * 16 + (code >> 9)
    lo = code & 127
    at_hi = (iota((128, 512), 0) == hi).astype(f32)
    at_lo = iota((128, 512), 0) == lo
    field = jnp.concatenate([density[:, c * 128 : (c + 1) * 128] for c in range(4)] + [jnp.zeros((64, 128), f32)], axis=0)
    picked = dot(jnp.transpose(field), at_hi)
    rho = jnp.sum(jnp.where(at_lo, picked, 0.0), axis=0, keepdims=True)
    answer = 2.0 - rho
    spread = jnp.where(at_lo, 0.5 * coef * answer, 0.0)
    total = dot_t(at_hi, spread)
    source = jnp.concatenate([total[c * 16 : (c + 1) * 16, :] for c in range(4)], axis=1)
    reply = jnp.concatenate([answer[:, k * 128 : (k + 1) * 128] for k in range(4)] + [jnp.zeros((124, 128), f32)], axis=0)
    return jnp.transpose(reply), source


def read_reply(reply, named, rank):
    rows = jnp.transpose(reply)[0:8, :]
    got = dot(rows, named)
    return jnp.sum(jnp.where(iota((8, 256), 0) == rank, got, 0.0), axis=0, keepdims=True)


VELOCITIES = [
    (0, 0, 0),
    (1, 0, 0),
    (-1, 0, 0),
    (0, 1, 0),
    (0, -1, 0),
    (0, 0, 1),
    (0, 0, -1),
    (1, 1, 0),
    (-1, -1, 0),
    (1, -1, 0),
    (-1, 1, 0),
    (1, 0, 1),
    (-1, 0, -1),
    (1, 0, -1),
    (-1, 0, 1),
    (0, 1, 1),
    (0, -1, -1),
    (0, 1, -1),
    (0, -1, 1),
    (0, 0, 0),
]
FLAG = 19
UP = [q for q in range(19) if VELOCITIES[q][0] == 1]
FLAT = [q for q in range(20) if VELOCITIES[q][0] == 0]
DOWN = [q for q in range(19) if VELOCITIES[q][0] == -1]
ZPLACE = {q: i for i, q in enumerate(UP + FLAT + DOWN)}
XUP = [q for q in range(19) if VELOCITIES[q][1] == 1]
XFLAT = [q for q in range(20) if VELOCITIES[q][1] == 0]
XDOWN = [q for q in range(19) if VELOCITIES[q][1] == -1]
XTILES = XUP + XUP[-1:] + XFLAT + XDOWN + XDOWN[-1:]
XPLACE = {q: XTILES.index(q) for q in range(20)}
NEAR = [(a, b) for a in (-1, 0, 1) for b in (-1, 0, 1) if (a, b) != (0, 0)]
ASIDE = [(a, b) for a, b in NEAR if b != 0]


def dotc(c, v):
    total = None
    for k, x in zip(c, v):
        if k:
            total = (x if k > 0 else -x) if total is None else (total + x if k > 0 else total - x)
    return total


def total_of(terms):
    out = terms[0]
    for t in terms[1:]:
        out = out + t
    return out


def density_of(g):
    near = total_of([g[q] for q in range(1, 7)])
    far = total_of([g[q] for q in range(7, 19)])
    return g[0] * (1.0 / 3.0) + near * (1.0 / 18.0) + far * (1.0 / 36.0)


def collide(g, solid, source, wanted):
    diff = {q: g[q] - g[q + 1] for q in range(1, 19, 2)}
    rho = density_of(g)
    j = []
    for axis in range(3):
        far = None
        for q in range(7, 19, 2):
            k = VELOCITIES[q][axis]
            if k:
                far = diff[q] if far is None else (far + diff[q] if k > 0 else far - diff[q])
        j.append(diff[1 + 2 * axis] * (4.8 / 18.0) + far * (4.8 / 36.0))
    scale = (1.5 / 4.8) / rho
    u = [x * scale for x in j]
    own = [x * y for x, y in zip(j, u)]
    base = 1.6 * rho - (own[0] + own[1] + own[2]) * (1.0 / 3.0)
    if source is not None:
        base = base + source
    out = {}
    if 0 in wanted:
        out[0] = jnp.where(solid, g[0], base - 0.6 * g[0])
    for q in range(1, 19, 2):
        if q not in wanted and q + 1 not in wanted:
            continue
        odd = dotc(VELOCITIES[q], j)
        even = base + (own[q // 2] if q < 7 else odd * dotc(VELOCITIES[q], u))
        if q in wanted:
            out[q] = jnp.where(solid, g[q + 1], even + odd - 0.6 * g[q])
        if q + 1 in wanted:
            out[q + 1] = jnp.where(solid, g[q], even - odd - 0.6 * g[q + 1])
    return out, rho


def wide(ref, q, rows):
    return jnp.concatenate([ref[q, c, rows, :] for c in range(4)], axis=1)


def put(ref, q, rows, value):
    for c in range(4):
        ref[q, c, rows, :] = value[:, 128 * c : 128 * c + 128]


def lane_roll(x, cy):
    return x if cy == 0 else pltpu.roll(x, cy % 512, 1)


def row_roll(x, k):
    return pltpu.roll(x, k % x.shape[0], 0)


def remote(src, dst, send, recv, gz, col):
    return pltpu.make_async_remote_copy(
        src_ref=src, dst_ref=dst, send_sem=send, recv_sem=recv, device_id={"gz": gz, "col": col}, device_id_type=MESH
    )


def step_pair(own, vox, rad, rate, ice, solid, pops, out, answer, coefs, ices, *scratch):
    (own_v, vox_v, rad_v, rate_v, solid_v, pops_v, ask, asked, tell, told, rel, below, above, edge, left, right) = scratch[:16]
    (src, near, spread, work, post, dens, loads, sends, recvs, zsend, zrecv, xsend, xrecv, nsend, nrecv) = scratch[16:]
    gz, col = lax.axis_index("gz"), lax.axis_index("col")
    z, d = gz // 16, lax.rem(gz, 16)
    barrier = pltpu.get_barrier_semaphore()

    fetch = [
        pltpu.make_async_copy(a, b, loads.at[i])
        for i, (a, b) in enumerate(
            [(own, own_v), (vox, vox_v), (rad, rad_v), (rate, rate_v), (ice, ices), (solid, solid_v), (pops, pops_v)]
        )
    ]
    for c in fetch:
        c.start()
    greet_group(barrier, z, d)

    def beside(dz, dx):
        return lax.rem(gz + dz + 128, 128), lax.rem(col + dx + 4, 4)

    for dz, dx in ASIDE:
        g, c = beside(dz, dx)
        pl.semaphore_signal(barrier, inc=1, device_id={"gz": g, "col": c}, device_id_type=MESH)
    for c in fetch:
        c.wait()
    table, named, rank, coef = request_table(own_v, vox_v, rad_v, rate_v, z, d)
    ask[...] = table
    coefs[0:1, :] = coef[:, 0:128]
    coefs[1:2, :] = coef[:, 128:256]

    def first(i, carry):
        lanes = pl.ds(pl.multiple_of(i * 128, 128), 128)
        g = [pops_v[q, :, lanes].astype(f32) for q in range(19)]
        made, rho = collide(g, solid_v[:, lanes] > 0, None, range(19))
        dens[:, lanes] = rho
        for q in range(19):
            post[q, i, 0:16, :] = made[q]
        return carry

    lax.fori_loop(0, 4, first, 0)
    for q in range(19):
        rel[ZPLACE[q]] = lane_roll(wide(post, q, pl.ds(0, 16)), VELOCITIES[q][2]).astype(bf16)
    rel[ZPLACE[FLAG]] = jnp.where(solid_v[...] > 0, 1.0, 0.0).astype(bf16)

    pl.semaphore_wait(barrier, 127 + len(ASIDE))
    up, down = beside(1, 0), beside(-1, 0)
    zcopies = [
        remote(rel.at[pl.ds(0, 15)], below, zsend.at[0], zrecv.at[0], *up),
        remote(rel.at[pl.ds(5, 15)], above, zsend.at[1], zrecv.at[1], *down),
    ]
    send_rows(ask, asked, sends.at[0], recvs.at[0], z, d, 1)
    asked[0:1, :] = ask[0:1, :]
    for c in zcopies:
        c.start()

    for c in zcopies:
        c.wait_recv()
    has_below, has_above = gz > 0, gz < 127
    for q in range(20):
        cz, i = VELOCITIES[q][0], ZPLACE[q]
        mine = rel[i].astype(f32)
        if cz >= 0:
            under = jnp.where(has_below, below[i].astype(f32), 0.0)
        if cz <= 0:
            over = jnp.where(has_above, above[i - 5].astype(f32), 0.0)
        if cz == 1:
            rows = [under, mine]
        elif cz == -1:
            rows = [mine, over]
        else:
            rows = [under[8:16], mine, over[0:8]]
        put(work, q, pl.ds(0, 32), jnp.concatenate(rows, axis=0))

    def column(q, x):
        return wide(work, q, pl.ds(x, 4, stride=8))

    def edge_tile(q):
        cx = VELOCITIES[q][1]
        first_x, then_x = {0: (7, 0), 1: (7, 6), -1: (0, 1)}[cx]
        return jnp.concatenate([column(q, first_x), column(q, then_x)], axis=0)

    for b in range(11):
        edge[b] = jnp.concatenate([edge_tile(XTILES[2 * b]), edge_tile(XTILES[2 * b + 1])], axis=0).astype(bf16)
    to_right, to_left = beside(0, 1), beside(0, -1)
    xcopies = [
        remote(edge.at[pl.ds(0, 8)], left, xsend.at[0], xrecv.at[0], *to_right),
        remote(edge.at[pl.ds(3, 8)], right, xsend.at[1], xrecv.at[1], *to_left),
    ]
    for c in xcopies:
        c.start()

    wait_rows(asked, recvs.at[0])
    reply, total = serve(asked[...], dens[...])
    src[...] = jnp.where(solid_v[...] > 0, 0.0, total).astype(bf16)
    ncopies = []
    for i, (dz, dx) in enumerate(NEAR):
        ncopies.append(remote(src, near.at[7 - i], nsend.at[i], nrecv.at[7 - i], *beside(dz, dx)))
    for c in ncopies:
        c.start()
    tell[...] = reply
    send_rows(tell, told, sends.at[1], recvs.at[1], z, d, -1)
    told[0:1, :] = tell[0:1, :]

    for c in xcopies:
        c.wait_recv()
    has_left, has_right = col > 0, col < 3
    row8 = iota((8, 512), 0)

    def tile(ref, shift, q, there):
        k = XPLACE[q] - shift
        both = jnp.where(there, ref[k // 2].astype(f32), 0.0)
        return both[8 * (k % 2) : 8 * (k % 2) + 8]

    for q in range(20):
        cx = VELOCITIES[q][1]
        if cx == 0:
            put(work, q, pl.ds(32, 8), jnp.where(row8 < 4, tile(left, 0, q, has_left), tile(right, 6, q, has_right)))
        else:
            ends = tile(left, 0, q, has_left) if cx == 1 else tile(right, 6, q, has_right)
            k = XPLACE[q]
            mine = edge[k // 2].astype(f32)[8 * (k % 2) : 8 * (k % 2) + 8]
            merged = jnp.where(row8 < 4, mine, ends)
            put(work, q, pl.ds(32, 8), row_roll(merged, 4) if cx == 1 else merged)
            put(work, q, pl.ds(0, 32), row_roll(wide(work, q, pl.ds(0, 32)), cx))
            put(work, q, pl.ds(0 if cx == 1 else 7, 4, stride=8), ends[0:4])

    for i in range(8):
        remote(src, near.at[i], nsend.at[7 - i], nrecv.at[i], gz, col).wait_recv()
    for a in (-1, 0, 1):
        for b in (-1, 0, 1):
            there = True
            if (a, b) == (0, 0):
                block = src[...].astype(f32)
            else:
                block = near[NEAR.index((a, b))].astype(f32)
                if a:
                    there = has_below if a < 0 else has_above
                if b:
                    sideways = has_left if b < 0 else has_right
                    there = jnp.logical_and(there, sideways) if a else sideways
                block = jnp.where(there, block, 0.0)
            for k in (0, 1):
                plane = block[8 * k : 8 * k + 8]
                at = 16 * (2 * (a + 1) + k)
                for cy in (-1, 0, 1):
                    moved = lane_roll(plane, cy)
                    if b == 0:
                        put(spread, cy + 1, pl.ds(at + 2, 8), moved)
                    elif b < 0:
                        put(spread, cy + 1, pl.ds(at, 2), moved[6:8])
                    else:
                        put(spread, cy + 1, pl.ds(at + 10, 2), moved[0:2])
    for q in range(20):
        cz, cx, cy = VELOCITIES[q]
        rows = [pl.ds(16 * (p + 1 - cz) + 2 - cx, 8) for p in range(4)]
        rows += [pl.ds(16 * (1 - cz) + k - cx, 4, stride=16) for k in (1, 10)]
        for c in range(4):
            added = jnp.concatenate([spread[cy + 1, c, r, :] for r in rows], axis=0)
            if q == FLAG:
                post[FLAG, c] = added
            else:
                work[q, c] = (work[q, c] + added).astype(bf16).astype(f32)

    row = iota((8, 128), 0)
    plane_in = jnp.logical_and(
        jnp.logical_or((row & 3) != 0, has_below), jnp.logical_or((row & 3) != 3, has_above)
    )
    side_in = jnp.logical_or(jnp.logical_and(row < 4, has_left), jnp.logical_and(row >= 4, has_right))
    edge_in = jnp.logical_and(plane_in, side_in)
    jobs = [(8, range(19), None), (16, range(19), None), (0, UP, has_below), (24, DOWN, has_above), (32, XUP + XDOWN, edge_in)]

    def second(i, carry):
        for r, wanted, inside in jobs:
            rows = pl.ds(r, 8)
            g = [work[q, i, rows, :] for q in range(19)]
            made, _ = collide(g, work[FLAG, i, rows, :] > 0.5, post[FLAG, i, rows, :], wanted)
            for q in wanted:
                post[q, i, rows, :] = made[q] if inside is None else jnp.where(inside, made[q], 0.0)
        return carry

    lax.fori_loop(0, 4, second, 0)
    for q in range(19):
        cz, cx, cy = VELOCITIES[q]
        r = 8 * (1 - cz)
        moved = wide(post, q, pl.ds(r, 16))
        if cx:
            moved = row_roll(moved, cx)
            rim = 32 + (1 - cz) if cx == 1 else 36 + (1 - cz)
            for k in (0, 1):
                at = 8 * k + (0 if cx == 1 else 7)
                moved = jnp.where(iota((16, 512), 0) == at, wide(post, q, pl.ds(rim + k, 1)), moved)
        out[q] = lane_roll(moved, cy).astype(bf16)

    wait_rows(told, recvs.at[1])
    line = read_reply(told[...], named, rank)
    answer[0:1, :] = line[:, 0:128]
    answer[1:2, :] = line[:, 128:256]
    wait_rows(ask, sends.at[0])
    wait_rows(tell, sends.at[1])
    for c in zcopies + xcopies + ncopies:
        c.wait_send()


def body(populations, solid, radius, rate, ice_mass, owner, voxel):
    vm = pl.BlockSpec(memory_space=pltpu.VMEM)
    hbm = pl.BlockSpec(memory_space=pltpu.HBM)
    sem = pltpu.SemaphoreType.DMA
    pair = jax.ShapeDtypeStruct((2, 128), f32)
    small = [pltpu.VMEM((2, 128), jnp.int32)] * 2 + [pltpu.VMEM((2, 128), f32)] * 2
    operands = [x.reshape(2, 128) for x in (owner, voxel, radius, rate, ice_mass)]
    operands += [solid.reshape(16, 512), populations.reshape(19, 16, 512)]
    state, answer, coef, ice = pl.pallas_call(
        step_pair,
        out_shape=(jax.ShapeDtypeStruct((19, 16, 512), bf16), pair, pair, pair),
        in_specs=[hbm] * 7,
        out_specs=(vm,) * 4,
        scratch_shapes=small
        + [pltpu.VMEM((16, 512), jnp.int32), pltpu.VMEM((19, 16, 512), bf16)]
        + [pltpu.VMEM((128, 128), f32)] * 4
        + [pltpu.VMEM((20, 16, 512), bf16)]
        + [pltpu.VMEM((15, 16, 512), bf16)] * 2
        + [pltpu.VMEM((11, 16, 512), bf16)]
        + [pltpu.VMEM((8, 16, 512), bf16)] * 2
        + [pltpu.VMEM((16, 512), bf16), pltpu.VMEM((8, 16, 512), bf16)]
        + [pltpu.VMEM((3, 4, 96, 128), f32)]
        + [pltpu.VMEM((20, 4, 40, 128), f32)] * 2
        + [pltpu.VMEM((16, 512), f32)]
        + [sem((7,))]
        + [sem((2,))] * 6
        + [sem((8,))] * 2,
        name="two_steps",
        compiler_params=pltpu.CompilerParams(collective_id=0, has_side_effects=True, vmem_limit_bytes=48 * 2**20),
    )(*[pltpu.with_memory_space_constraint(x, pltpu.HBM) for x in operands])
    flux = coef * answer
    return (state.reshape(populations.shape), flux.reshape(-1), (ice - flux).reshape(-1))


def solution(mesh):
    return jax.shard_map(
        body,
        mesh=mesh,
        in_specs=(
            P(None, "gz", "col", None),
            P("gz", "col", None),
            P(("gz", "col")),
            P(("gz", "col")),
            P(("gz", "col")),
            P(("gz", "col"), None),
            P(("gz", "col")),
        ),
        out_specs=(P(None, "gz", "col", None), P(("gz", "col")), P(("gz", "col"))),
        check_vma=False,
    )
```

```python
import jax
import jax.numpy as jnp
from jax import lax
from jax.experimental import pallas as pl
from jax.experimental.pallas import tpu as pltpu
from jax.sharding import PartitionSpec as P

MESH = pl.DeviceIdType.MESH
HIGHEST = lax.Precision.HIGHEST
f32 = jnp.float32
bf16 = jnp.bfloat16


def hops(pair):
    o, e = pair
    return min(o, 8 - o) + min(e, 16 - e) / 2


PEERS = sorted([(o, e) for o in range(8) for e in range(16) if (o, e) != (0, 0)], key=lambda p: -hops(p))

FAR = [p for p in PEERS if hops(p) >= 4.5]
CLOSE = [p for p in PEERS if hops(p) < 4.5]


def peer(z, d, o, e):
    return lax.rem(z + o, 8) * 16 + lax.rem(d + e, 16)


def greet_group(sem, z, d):
    for o, e in PEERS:
        pl.semaphore_signal(sem, inc=1, device_id={"gz": peer(z, d, o, e)}, device_id_type=MESH)


def send_rows(src, dst, send, recv, z, d, sign, peers):
    for o, e in peers:
        row = pl.ds(o * 16 + e, 1)
        to = peer(z, d, o, e) if sign > 0 else peer(z, d, (8 - o) % 8, (16 - e) % 16)
        pltpu.make_async_remote_copy(
            src_ref=src.at[row],
            dst_ref=dst.at[row],
            send_sem=send,
            recv_sem=recv,
            device_id={"gz": to},
            device_id_type=MESH,
        ).start()


def wait_rows(buf, sem):
    rows = buf.at[pl.ds(1, 127)]
    pltpu.make_async_copy(rows, rows, sem).wait()


def iota(shape, dim):
    return lax.broadcasted_iota(jnp.int32, shape, dim)


def flat_row(ref):
    return jnp.concatenate([ref[0:1, :], ref[1:2, :]], axis=1)


def dot_t(a, b):
    return lax.dot_general(a, b, (((1,), (1,)), ((), ())), precision=HIGHEST, preferred_element_type=f32)


def dot(a, b):
    return jnp.dot(a, b, precision=HIGHEST, preferred_element_type=f32)


def request_table(own_ref, vox_ref, rad_ref, rate_ref, z, d):
    own, vox = flat_row(own_ref), flat_row(vox_ref)
    rad, rate = flat_row(rad_ref), flat_row(rate_ref)
    coef = rate * rad * rad
    rel = (((own >> 4) - z) & 7) * 16 + (((own & 15) - d) & 15)
    named = (iota((128, 256), 0) == rel).astype(f32)
    earlier = (iota((256, 256), 0) < iota((256, 256), 1)).astype(bf16)
    before = jnp.dot(named.astype(bf16), earlier, preferred_element_type=f32)
    rank = jnp.sum(before * named, axis=0, keepdims=True).astype(jnp.int32)
    lane = iota((128, 256), 0)
    value = jnp.where(lane < 4, coef, jnp.where(lane < 8, vox.astype(f32), 0.0))
    value = jnp.where((lane & 3) == rank, value, 0.0)
    return dot_t(named, value), named, rank, coef


def parts(x):
    high = x.astype(bf16)
    rest = x - high.astype(f32)
    middle = rest.astype(bf16)
    return [high, middle, (rest - middle.astype(f32)).astype(bf16)]


def lookup_field(density):
    field = jnp.concatenate([density[:, c * 128 : (c + 1) * 128] for c in range(4)], axis=0)
    return jnp.concatenate(parts(jnp.transpose(field)), axis=1)


def look_up(table, field):
    rows = jnp.transpose(table)
    coef = jnp.concatenate([rows[k : k + 1, :] for k in range(4)], axis=1)
    code = jnp.concatenate([rows[k : k + 1, :] for k in range(4, 8)], axis=1).astype(jnp.int32)
    hi = ((code >> 7) & 3) * 16 + (code >> 9)
    at_lo = iota((128, 512), 0) == (code & 127)
    at_hi = ((iota((192, 512), 0) & 63) == hi).astype(f32).astype(bf16)
    picked = jnp.dot(field, at_hi, preferred_element_type=f32)
    answer = 2.0 - jnp.sum(jnp.where(at_lo, picked, 0.0), axis=0, keepdims=True)
    reply = jnp.concatenate([answer[:, k * 128 : (k + 1) * 128] for k in range(4)] + [jnp.zeros((4, 128), f32)], axis=0)
    return jnp.transpose(reply), (coef * answer, at_lo, at_hi[0:64])


def scatter(flux, at_lo, at_hi):
    spread = jnp.concatenate(parts(jnp.where(at_lo, 0.5 * flux, 0.0)), axis=1)
    where = jnp.concatenate([at_hi] * 3, axis=1)
    total = lax.dot_general(where, spread, (((1,), (1,)), ((), ())), preferred_element_type=f32)
    return jnp.concatenate([total[c * 16 : (c + 1) * 16, :] for c in range(4)], axis=1)


def read_reply(reply, named, rank):
    rows = jnp.transpose(reply)
    got = jnp.dot(jnp.concatenate(parts(rows), axis=0), named, preferred_element_type=f32)
    got = got[0:8] + got[8:16] + got[16:24]
    return jnp.sum(jnp.where(iota((8, 256), 0) == rank, got, 0.0), axis=0, keepdims=True)


VELOCITIES = [
    (0, 0, 0),
    (1, 0, 0),
    (-1, 0, 0),
    (0, 1, 0),
    (0, -1, 0),
    (0, 0, 1),
    (0, 0, -1),
    (1, 1, 0),
    (-1, -1, 0),
    (1, -1, 0),
    (-1, 1, 0),
    (1, 0, 1),
    (-1, 0, -1),
    (1, 0, -1),
    (-1, 0, 1),
    (0, 1, 1),
    (0, -1, -1),
    (0, 1, -1),
    (0, -1, 1),
    (0, 0, 0),
]
FLAG = 19
UP = [q for q in range(19) if VELOCITIES[q][0] == 1]
FLAT = [q for q in range(20) if VELOCITIES[q][0] == 0]
DOWN = [q for q in range(19) if VELOCITIES[q][0] == -1]
ZPLACE = {q: i for i, q in enumerate(UP + FLAT + DOWN)}
XUP = [q for q in range(19) if VELOCITIES[q][1] == 1]
XFLAT = [q for q in range(20) if VELOCITIES[q][1] == 0]
XDOWN = [q for q in range(19) if VELOCITIES[q][1] == -1]
XTILES = XUP + XUP[-1:] + XFLAT + XDOWN + XDOWN[-1:]
XPLACE = {q: XTILES.index(q) for q in range(20)}
NEAR = [(a, b) for a in (-1, 0, 1) for b in (-1, 0, 1) if (a, b) != (0, 0)]
ASIDE = [(a, b) for a, b in NEAR if b != 0]


def dotc(c, v):
    total = None
    for k, x in zip(c, v):
        if k:
            total = (x if k > 0 else -x) if total is None else (total + x if k > 0 else total - x)
    return total


def total_of(terms):
    out = terms[0]
    for t in terms[1:]:
        out = out + t
    return out


def density_of(g):
    near = total_of([g[q] for q in range(1, 7)])
    far = total_of([g[q] for q in range(7, 19)])
    return g[0] * (1.0 / 3.0) + near * (1.0 / 18.0) + far * (1.0 / 36.0)


def collide(g, solid, source, wanted):
    diff = {q: g[q] - g[q + 1] for q in range(1, 19, 2)}
    rho = density_of(g)
    j = []
    for axis in range(3):
        far = None
        for q in range(7, 19, 2):
            k = VELOCITIES[q][axis]
            if k:
                far = diff[q] if far is None else (far + diff[q] if k > 0 else far - diff[q])
        j.append(diff[1 + 2 * axis] * (4.8 / 18.0) + far * (4.8 / 36.0))
    scale = (1.5 / 4.8) / rho
    u = [x * scale for x in j]
    own = [x * y for x, y in zip(j, u)]
    base = 1.6 * rho - (own[0] + own[1] + own[2]) * (1.0 / 3.0)
    if source is not None:
        base = base + source
    out = {}
    if 0 in wanted:
        out[0] = jnp.where(solid, g[0], base - 0.6 * g[0])
    for q in range(1, 19, 2):
        if q not in wanted and q + 1 not in wanted:
            continue
        odd = dotc(VELOCITIES[q], j)
        even = base + (own[q // 2] if q < 7 else odd * dotc(VELOCITIES[q], u))
        if q in wanted:
            out[q] = jnp.where(solid, g[q + 1], even + odd - 0.6 * g[q])
        if q + 1 in wanted:
            out[q + 1] = jnp.where(solid, g[q], even - odd - 0.6 * g[q + 1])
    return out, rho


def wide(ref, q, rows):
    return jnp.concatenate([ref[q, c, rows, :] for c in range(4)], axis=1)


def put(ref, q, rows, value):
    for c in range(4):
        ref[q, c, rows, :] = value[:, 128 * c : 128 * c + 128]


def lane_roll(x, cy):
    return x if cy == 0 else pltpu.roll(x, cy % 512, 1)


def row_roll(x, k):
    return pltpu.roll(x, k % x.shape[0], 0)


def remote(src, dst, send, recv, gz, col):
    return pltpu.make_async_remote_copy(
        src_ref=src, dst_ref=dst, send_sem=send, recv_sem=recv, device_id={"gz": gz, "col": col}, device_id_type=MESH
    )


def step_pair(own, vox, rad, rate, ice, solid, pops, out, flux, ice_left, *scratch):
    (own_v, vox_v, rad_v, rate_v, ice_v, solid_v, pops_v, ask, asked, tell, told, rel, below, above, edge, left, right) = scratch[:17]
    (src, near, spread, work, post, dens, field, named_ref, loads, sends, recvs, zsend, zrecv, xsend, xrecv, nsend, nrecv) = scratch[17:]
    gz, col = lax.axis_index("gz"), lax.axis_index("col")
    z, d = gz // 16, lax.rem(gz, 16)
    barrier = pltpu.get_barrier_semaphore()

    fetch = [
        pltpu.make_async_copy(a, b, loads.at[i])
        for i, (a, b) in enumerate(
            [(own, own_v), (vox, vox_v), (rad, rad_v), (rate, rate_v), (ice, ice_v), (solid, solid_v), (pops, pops_v)]
        )
    ]
    for c in fetch:
        c.start()
    greet_group(barrier, z, d)

    def beside(dz, dx):
        return lax.rem(gz + dz + 128, 128), lax.rem(col + dx + 4, 4)

    for dz, dx in ASIDE:
        g, c = beside(dz, dx)
        pl.semaphore_signal(barrier, inc=1, device_id={"gz": g, "col": c}, device_id_type=MESH)
    for c in fetch:
        c.wait()
    table, named, rank, coef = request_table(own_v, vox_v, rad_v, rate_v, z, d)
    ask[...] = table
    named_ref[...] = named.astype(bf16)

    def first(i, carry):
        lanes = pl.ds(pl.multiple_of(i * 128, 128), 128)
        g = [pops_v[q, :, lanes].astype(f32) for q in range(19)]
        made, rho = collide(g, solid_v[:, lanes] > 0, None, range(19))
        dens[:, lanes] = rho
        for q in range(19):
            post[q, i, 0:16, :] = made[q]
        return carry

    lax.fori_loop(0, 4, first, 0)
    field[...] = lookup_field(dens[...])
    for q in range(19):
        rel[ZPLACE[q]] = lane_roll(wide(post, q, pl.ds(0, 16)), VELOCITIES[q][2]).astype(bf16)
    rel[ZPLACE[FLAG]] = jnp.where(solid_v[...] > 0, 1.0, 0.0).astype(bf16)

    pl.semaphore_wait(barrier, 127 + len(ASIDE))
    up, down = beside(1, 0), beside(-1, 0)
    zcopies = [
        remote(rel.at[pl.ds(0, 15)], below, zsend.at[0], zrecv.at[0], *up),
        remote(rel.at[pl.ds(5, 15)], above, zsend.at[1], zrecv.at[1], *down),
    ]
    send_rows(ask, asked, sends.at[0], recvs.at[0], z, d, 1, PEERS)
    asked[0:1, :] = ask[0:1, :]
    for c in zcopies:
        c.start()

    for c in zcopies:
        c.wait_recv()
    has_below, has_above = gz > 0, gz < 127
    for q in range(20):
        cz, i = VELOCITIES[q][0], ZPLACE[q]
        mine = rel[i].astype(f32)
        if cz >= 0:
            under = jnp.where(has_below, below[i].astype(f32), 0.0)
        if cz <= 0:
            over = jnp.where(has_above, above[i - 5].astype(f32), 0.0)
        if cz == 1:
            rows = [under, mine]
        elif cz == -1:
            rows = [mine, over]
        else:
            rows = [under[8:16], mine, over[0:8]]
        put(work, q, pl.ds(0, 32), jnp.concatenate(rows, axis=0))

    def column(q, x):
        return wide(work, q, pl.ds(x, 4, stride=8))

    def edge_tile(q):
        cx = VELOCITIES[q][1]
        first_x, then_x = {0: (7, 0), 1: (7, 6), -1: (0, 1)}[cx]
        return jnp.concatenate([column(q, first_x), column(q, then_x)], axis=0)

    for b in range(11):
        edge[b] = jnp.concatenate([edge_tile(XTILES[2 * b]), edge_tile(XTILES[2 * b + 1])], axis=0).astype(bf16)
    to_right, to_left = beside(0, 1), beside(0, -1)
    xcopies = [
        remote(edge.at[pl.ds(0, 8)], left, xsend.at[0], xrecv.at[0], *to_right),
        remote(edge.at[pl.ds(3, 8)], right, xsend.at[1], xrecv.at[1], *to_left),
    ]
    for c in xcopies:
        c.start()

    wait_rows(asked, recvs.at[0])
    reply, slots = look_up(asked[:, 0:8], field[...])
    tell[:, 0:8] = reply
    send_rows(tell, told, sends.at[1], recvs.at[1], z, d, -1, FAR)
    total = scatter(*slots)
    src[...] = jnp.where(solid_v[...] > 0, 0.0, total).astype(bf16)
    ncopies = []
    for i, (dz, dx) in enumerate(NEAR):
        ncopies.append(remote(src, near.at[7 - i], nsend.at[i], nrecv.at[7 - i], *beside(dz, dx)))
    for c in ncopies:
        c.start()
    send_rows(tell, told, sends.at[1], recvs.at[1], z, d, -1, CLOSE)
    told[0:1, :] = tell[0:1, :]

    for c in xcopies:
        c.wait_recv()
    has_left, has_right = col > 0, col < 3
    row8 = iota((8, 512), 0)

    def tile(ref, shift, q, there):
        k = XPLACE[q] - shift
        both = jnp.where(there, ref[k // 2].astype(f32), 0.0)
        return both[8 * (k % 2) : 8 * (k % 2) + 8]

    for q in range(20):
        cx = VELOCITIES[q][1]
        if cx == 0:
            put(work, q, pl.ds(32, 8), jnp.where(row8 < 4, tile(left, 0, q, has_left), tile(right, 6, q, has_right)))
        else:
            ends = tile(left, 0, q, has_left) if cx == 1 else tile(right, 6, q, has_right)
            k = XPLACE[q]
            mine = edge[k // 2].astype(f32)[8 * (k % 2) : 8 * (k % 2) + 8]
            merged = jnp.where(row8 < 4, mine, ends)
            put(work, q, pl.ds(32, 8), row_roll(merged, 4) if cx == 1 else merged)
            put(work, q, pl.ds(0, 32), row_roll(wide(work, q, pl.ds(0, 32)), cx))
            put(work, q, pl.ds(0 if cx == 1 else 7, 4, stride=8), ends[0:4])

    for i in range(8):
        remote(src, near.at[i], nsend.at[7 - i], nrecv.at[i], gz, col).wait_recv()
    for a in (-1, 0, 1):
        for b in (-1, 0, 1):
            there = True
            if (a, b) == (0, 0):
                block = src[...].astype(f32)
            else:
                block = near[NEAR.index((a, b))].astype(f32)
                if a:
                    there = has_below if a < 0 else has_above
                if b:
                    sideways = has_left if b < 0 else has_right
                    there = jnp.logical_and(there, sideways) if a else sideways
                block = jnp.where(there, block, 0.0)
            for k in (0, 1):
                plane = block[8 * k : 8 * k + 8]
                at = 16 * (2 * (a + 1) + k)
                for cy in (-1, 0, 1):
                    moved = lane_roll(plane, cy)
                    if b == 0:
                        put(spread, cy + 1, pl.ds(at + 2, 8), moved)
                    elif b < 0:
                        put(spread, cy + 1, pl.ds(at, 2), moved[6:8])
                    else:
                        put(spread, cy + 1, pl.ds(at + 10, 2), moved[0:2])
    for q in range(20):
        cz, cx, cy = VELOCITIES[q]
        rows = [pl.ds(16 * (p + 1 - cz) + 2 - cx, 8) for p in range(4)]
        rows += [pl.ds(16 * (1 - cz) + k - cx, 4, stride=16) for k in (1, 10)]
        for c in range(4):
            added = jnp.concatenate([spread[cy + 1, c, r, :] for r in rows], axis=0)
            if q == FLAG:
                post[FLAG, c] = added
            else:
                work[q, c] = (work[q, c] + added).astype(bf16).astype(f32)

    row = iota((8, 128), 0)
    plane_in = jnp.logical_and(
        jnp.logical_or((row & 3) != 0, has_below), jnp.logical_or((row & 3) != 3, has_above)
    )
    side_in = jnp.logical_or(jnp.logical_and(row < 4, has_left), jnp.logical_and(row >= 4, has_right))
    edge_in = jnp.logical_and(plane_in, side_in)
    jobs = [(8, range(19), None), (16, range(19), None), (0, UP, has_below), (24, DOWN, has_above), (32, XUP + XDOWN, edge_in)]

    def second(i, carry):
        for r, wanted, inside in jobs:
            rows = pl.ds(r, 8)
            g = [work[q, i, rows, :] for q in range(19)]
            made, _ = collide(g, work[FLAG, i, rows, :] > 0.5, post[FLAG, i, rows, :], wanted)
            for q in wanted:
                post[q, i, rows, :] = made[q] if inside is None else jnp.where(inside, made[q], 0.0)
        return carry

    lax.fori_loop(0, 4, second, 0)
    for q in range(19):
        cz, cx, cy = VELOCITIES[q]
        r = 8 * (1 - cz)
        moved = wide(post, q, pl.ds(r, 16))
        if cx:
            moved = row_roll(moved, cx)
            rim = 32 + (1 - cz) if cx == 1 else 36 + (1 - cz)
            for k in (0, 1):
                at = 8 * k + (0 if cx == 1 else 7)
                moved = jnp.where(iota((16, 512), 0) == at, wide(post, q, pl.ds(rim + k, 1)), moved)
        out[q] = lane_roll(moved, cy).astype(bf16)

    wait_rows(told, recvs.at[1])
    line = coef * read_reply(told[:, 0:8], named_ref[...], rank)
    for k in (0, 1):
        row = line[:, 128 * k : 128 * k + 128]
        flux[k : k + 1, :] = row
        ice_left[k : k + 1, :] = ice_v[k : k + 1, :] - row
    wait_rows(ask, sends.at[0])
    wait_rows(tell, sends.at[1])
    for c in zcopies + xcopies + ncopies:
        c.wait_send()


def hand_over(a, b, c, x, y, z, sems):
    copies = [pltpu.make_async_copy(s, t, sems.at[i]) for i, (s, t) in enumerate([(a, x), (b, y), (c, z)])]
    for one in copies:
        one.start()
    for one in copies:
        one.wait()


def body(populations, solid, radius, rate, ice_mass, owner, voxel):
    vm = pl.BlockSpec(memory_space=pltpu.VMEM)
    hbm = pl.BlockSpec(memory_space=pltpu.HBM)
    sem = pltpu.SemaphoreType.DMA
    pair = jax.ShapeDtypeStruct((2, 128), f32)
    small = [pltpu.VMEM((2, 128), jnp.int32)] * 2 + [pltpu.VMEM((2, 128), f32)] * 3
    operands = [x.reshape(2, 128) for x in (owner, voxel, radius, rate, ice_mass)]
    operands += [solid.reshape(16, 512), populations.reshape(19, 16, 512)]
    moved = pl.pallas_call(
        step_pair,
        out_shape=(jax.ShapeDtypeStruct((19, 16, 512), bf16), pair, pair),
        in_specs=[hbm] * 7,
        out_specs=(vm,) * 3,
        scratch_shapes=small
        + [pltpu.VMEM((16, 512), jnp.int32), pltpu.VMEM((19, 16, 512), bf16)]
        + [pltpu.VMEM((128, 128), f32)] * 4
        + [pltpu.VMEM((20, 16, 512), bf16)]
        + [pltpu.VMEM((15, 16, 512), bf16)] * 2
        + [pltpu.VMEM((11, 16, 512), bf16)]
        + [pltpu.VMEM((8, 16, 512), bf16)] * 2
        + [pltpu.VMEM((16, 512), bf16), pltpu.VMEM((8, 16, 512), bf16)]
        + [pltpu.VMEM((3, 4, 96, 128), f32)]
        + [pltpu.VMEM((20, 4, 40, 128), f32)] * 2
        + [pltpu.VMEM((16, 512), f32), pltpu.VMEM((128, 192), bf16), pltpu.VMEM((128, 256), bf16)]
        + [sem((7,))]
        + [sem((2,))] * 6
        + [sem((8,))] * 2,
        name="two_steps",
        compiler_params=pltpu.CompilerParams(collective_id=0, has_side_effects=True, vmem_limit_bytes=48 * 2**20),
    )(*[pltpu.with_memory_space_constraint(x, pltpu.HBM) for x in operands])
    state, flux, ice_left = pl.pallas_call(
        hand_over,
        out_shape=(jax.ShapeDtypeStruct((19, 16, 512), bf16), pair, pair),
        in_specs=[vm] * 3,
        out_specs=(hbm,) * 3,
        scratch_shapes=[sem((3,))],
        name="hand_over",
        compiler_params=pltpu.CompilerParams(vmem_limit_bytes=4 * 2**20),
    )(*[pltpu.with_memory_space_constraint(x, pltpu.VMEM) for x in moved])
    return (state.reshape(populations.shape), flux.reshape(-1), ice_left.reshape(-1))


def solution(mesh):
    return jax.shard_map(
        body,
        mesh=mesh,
        in_specs=(
            P(None, "gz", "col", None),
            P("gz", "col", None),
            P(("gz", "col")),
            P(("gz", "col")),
            P(("gz", "col")),
            P(("gz", "col"), None),
            P(("gz", "col")),
        ),
        out_specs=(P(None, "gz", "col", None), P(("gz", "col")), P(("gz", "col"))),
        check_vma=False,
    )
```

```python
import jax
import jax.numpy as jnp
from jax import lax
from jax.experimental import pallas as pl
from jax.experimental.pallas import tpu as pltpu
from jax.sharding import PartitionSpec as P

MESH = pl.DeviceIdType.MESH
HIGHEST = lax.Precision.HIGHEST
f32 = jnp.float32
bf16 = jnp.bfloat16


def hops(pair):
    o, e = pair
    return min(o, 8 - o) + min(e, 16 - e) / 2


PEERS = sorted([(o, e) for o in range(8) for e in range(16) if (o, e) != (0, 0)], key=lambda p: -hops(p))

TURNS = sorted(range(16), key=lambda e: -min(e, 16 - e))


def peer(z, d, o, e):
    return lax.rem(z + o, 8) * 16 + lax.rem(d + e, 16)


def greet_group(sem, z, d):
    for o, e in PEERS:
        pl.semaphore_signal(sem, inc=1, device_id={"gz": peer(z, d, o, e)}, device_id_type=MESH)


def rows_of(place):
    return pl.ds(pl.multiple_of(2 * place, 2), 2)


def rows_copy(src, dst, send, recv, gz):
    return pltpu.make_async_remote_copy(
        src_ref=src, dst_ref=dst, send_sem=send, recv_sem=recv, device_id={"gz": gz}, device_id_type=MESH
    )


def wait_bytes(rows, sem):
    pltpu.make_async_copy(rows, rows, sem).wait()


def send_requests(ask, asked, send, recv, z, d):
    half, level = z // 4, lax.rem(z, 4)
    for e in TURNS:
        for there in range(4):
            src = ask.at[rows_of(there * 16 + e)]
            dst = asked.at[half, rows_of(level * 16 + e)]
            copy = rows_copy(src, dst, send, recv.at[half], there * 16 + lax.rem(d + e, 16))
            if e:
                copy.start()
            else:
                pl.when(z != there)(copy.start)
                pl.when(z == there)(pltpu.make_async_copy(src, dst, recv.at[half]).start)


def send_answers(tell, told, send, recv, half, z, d):
    for e in TURNS:
        for level in range(4):
            src = tell.at[half, rows_of(level * 16 + e)]
            dst = told.at[rows_of(z * 16 + e)]
            to = 4 * half + level
            copy = rows_copy(src, dst, send, recv, to * 16 + lax.rem(d + 16 - e, 16))
            if e or half:
                copy.start()
            else:
                pl.when(z != to)(copy.start)
                pl.when(z == to)(pltpu.make_async_copy(src, dst, recv).start)


def iota(shape, dim):
    return lax.broadcasted_iota(jnp.int32, shape, dim)


def flat_row(ref):
    return jnp.concatenate([ref[0:1, :], ref[1:2, :]], axis=1)


def dot_t(a, b):
    return lax.dot_general(a, b, (((1,), (1,)), ((), ())), precision=HIGHEST, preferred_element_type=f32)


def dot(a, b):
    return jnp.dot(a, b, precision=HIGHEST, preferred_element_type=f32)


def request_table(own_ref, vox_ref, rad_ref, rate_ref, d):
    own, vox = flat_row(own_ref), flat_row(vox_ref)
    rad, rate = flat_row(rad_ref), flat_row(rate_ref)
    coef = rate * rad * rad
    level, upper = own >> 4, own >> 6
    rel = 2 * (jnp.where(upper > 0, 7 - level, level) * 16 + (((own & 15) - d) & 15)) + upper
    named = (iota((128, 256), 0) == rel).astype(f32)
    earlier = (iota((256, 256), 0) < iota((256, 256), 1)).astype(bf16)
    before = jnp.dot(named.astype(bf16), earlier, preferred_element_type=f32)
    rank = jnp.sum(before * named, axis=0, keepdims=True).astype(jnp.int32)
    lane = iota((128, 256), 0)
    value = jnp.where(lane < 4, coef, jnp.where(lane < 8, vox.astype(f32), 0.0))
    value = jnp.where((lane & 3) == rank, value, 0.0)
    return dot_t(named, value), named, rank, coef


def parts(x):
    high = x.astype(bf16)
    rest = x - high.astype(f32)
    middle = rest.astype(bf16)
    return [high, middle, (rest - middle.astype(f32)).astype(bf16)]


def lookup_field(own, other):
    field = jnp.concatenate([x[:, c * 128 : (c + 1) * 128] for x in (own, other) for c in range(4)], axis=0)
    return jnp.concatenate(parts(jnp.transpose(field)), axis=1)


def look_up(table, field):
    rows = jnp.transpose(table)
    coef = jnp.concatenate([rows[k : k + 1, :] for k in range(4)], axis=1)
    code = jnp.concatenate([rows[k : k + 1, :] for k in range(4, 8)], axis=1).astype(jnp.int32)
    hi = (iota((1, 512), 1) & 1) * 64 + ((code >> 7) & 3) * 16 + (code >> 9)
    at_lo = iota((128, 512), 0) == (code & 127)
    at_hi = ((iota((384, 512), 0) & 127) == hi).astype(f32).astype(bf16)
    picked = jnp.dot(field, at_hi, preferred_element_type=f32)
    answer = 2.0 - jnp.sum(jnp.where(at_lo, picked, 0.0), axis=0, keepdims=True)
    reply = jnp.concatenate([answer[:, k * 128 : (k + 1) * 128] for k in range(4)] + [jnp.zeros((4, 128), f32)], axis=0)
    return jnp.transpose(reply), (coef * answer, at_lo, at_hi[0:128])


def scatter(flux, at_lo, at_hi):
    spread = jnp.concatenate(parts(jnp.where(at_lo, 0.5 * flux, 0.0)), axis=1)
    where = jnp.concatenate([at_hi] * 3, axis=1)
    return lax.dot_general(where, spread, (((1,), (1,)), ((), ())), preferred_element_type=f32)


def block_of(total, k):
    return jnp.concatenate([total[64 * k + 16 * c : 64 * k + 16 * c + 16, :] for c in range(4)], axis=1)


def read_reply(reply, named, rank):
    rows = jnp.transpose(reply)
    got = jnp.dot(jnp.concatenate(parts(rows), axis=0), named, preferred_element_type=f32)
    got = got[0:8] + got[8:16] + got[16:24]
    return jnp.sum(jnp.where(iota((8, 256), 0) == rank, got, 0.0), axis=0, keepdims=True)


VELOCITIES = [
    (0, 0, 0),
    (1, 0, 0),
    (-1, 0, 0),
    (0, 1, 0),
    (0, -1, 0),
    (0, 0, 1),
    (0, 0, -1),
    (1, 1, 0),
    (-1, -1, 0),
    (1, -1, 0),
    (-1, 1, 0),
    (1, 0, 1),
    (-1, 0, -1),
    (1, 0, -1),
    (-1, 0, 1),
    (0, 1, 1),
    (0, -1, -1),
    (0, 1, -1),
    (0, -1, 1),
    (0, 0, 0),
]
FLAG = 19
UP = [q for q in range(19) if VELOCITIES[q][0] == 1]
FLAT = [q for q in range(20) if VELOCITIES[q][0] == 0]
DOWN = [q for q in range(19) if VELOCITIES[q][0] == -1]
ZPLACE = {q: i for i, q in enumerate(UP + FLAT + DOWN)}
XUP = [q for q in range(19) if VELOCITIES[q][1] == 1]
XFLAT = [q for q in range(20) if VELOCITIES[q][1] == 0]
XDOWN = [q for q in range(19) if VELOCITIES[q][1] == -1]
XTILES = XUP + XUP[-1:] + XFLAT + XDOWN + XDOWN[-1:]
XPLACE = {q: XTILES.index(q) for q in range(20)}
NEAR = [(a, b) for a in (-1, 0, 1) for b in (-1, 0, 1) if (a, b) != (0, 0)]
ASIDE = [(a, b) for a, b in NEAR if b != 0]


def dotc(c, v):
    total = None
    for k, x in zip(c, v):
        if k:
            total = (x if k > 0 else -x) if total is None else (total + x if k > 0 else total - x)
    return total


def total_of(terms):
    out = terms[0]
    for t in terms[1:]:
        out = out + t
    return out


def density_of(g):
    near = total_of([g[q] for q in range(1, 7)])
    far = total_of([g[q] for q in range(7, 19)])
    return g[0] * (1.0 / 3.0) + near * (1.0 / 18.0) + far * (1.0 / 36.0)


def collide(g, solid, source, wanted):
    diff = {q: g[q] - g[q + 1] for q in range(1, 19, 2)}
    rho = density_of(g)
    j = []
    for axis in range(3):
        far = None
        for q in range(7, 19, 2):
            k = VELOCITIES[q][axis]
            if k:
                far = diff[q] if far is None else (far + diff[q] if k > 0 else far - diff[q])
        j.append(diff[1 + 2 * axis] * (4.8 / 18.0) + far * (4.8 / 36.0))
    scale = (1.5 / 4.8) / rho
    u = [x * scale for x in j]
    own = [x * y for x, y in zip(j, u)]
    base = 1.6 * rho - (own[0] + own[1] + own[2]) * (1.0 / 3.0)
    if source is not None:
        base = base + source
    out = {}
    if 0 in wanted:
        out[0] = jnp.where(solid, g[0], base - 0.6 * g[0])
    for q in range(1, 19, 2):
        if q not in wanted and q + 1 not in wanted:
            continue
        odd = dotc(VELOCITIES[q], j)
        even = base + (own[q // 2] if q < 7 else odd * dotc(VELOCITIES[q], u))
        if q in wanted:
            out[q] = jnp.where(solid, g[q + 1], even + odd - 0.6 * g[q])
        if q + 1 in wanted:
            out[q + 1] = jnp.where(solid, g[q], even - odd - 0.6 * g[q + 1])
    return out


def wide(ref, q, rows):
    return jnp.concatenate([ref[q, c, rows, :] for c in range(4)], axis=1)


def put(ref, q, rows, value):
    for c in range(4):
        ref[q, c, rows, :] = value[:, 128 * c : 128 * c + 128]


def lane_roll(x, cy):
    return x if cy == 0 else pltpu.roll(x, cy % 512, 1)


def row_roll(x, k):
    return pltpu.roll(x, k % x.shape[0], 0)


def remote(src, dst, send, recv, gz, col):
    return pltpu.make_async_remote_copy(
        src_ref=src, dst_ref=dst, send_sem=send, recv_sem=recv, device_id={"gz": gz, "col": col}, device_id_type=MESH
    )


def step_pair(own, vox, rad, rate, ice, solid, pops, out, flux, ice_left, *scratch):
    (own_v, vox_v, rad_v, rate_v, ice_v, solid_v, pops_v, ask, asked, told, tell, rel, below, above, edge, left, right) = scratch[:17]
    (src, near, spread, work, post, dens, named_ref, mdens, total, msrc, gsrc) = scratch[17:28]
    (loads, ask_send, ask_recv, tell_send, tell_recv, pair_send, pair_recv, zsend, zrecv, xsend, xrecv, nsend, nrecv) = scratch[28:]
    gz, col = lax.axis_index("gz"), lax.axis_index("col")
    z, d = gz // 16, lax.rem(gz, 16)
    barrier = pltpu.get_barrier_semaphore()

    fetch = [
        pltpu.make_async_copy(a, b, loads.at[i])
        for i, (a, b) in enumerate(
            [(own, own_v), (vox, vox_v), (rad, rad_v), (rate, rate_v), (ice, ice_v), (solid, solid_v), (pops, pops_v)]
        )
    ]
    for c in fetch:
        c.start()
    server, partner = z < 4, (7 - z) * 16 + d

    def beside(dz, dx):
        return lax.rem(gz + dz + 128, 128), lax.rem(col + dx + 4, 4)

    for dz, dx in NEAR:
        g, c = beside(dz, dx)
        pl.semaphore_signal(barrier, inc=1, device_id={"gz": g, "col": c}, device_id_type=MESH)

    @pl.when(server)
    def _():
        greet_group(barrier, z, d)

    for c in fetch[:5]:
        c.wait()
    table, named, rank, coef = request_table(own_v, vox_v, rad_v, rate_v, d)
    ask[...] = table
    named_ref[...] = named.astype(bf16)
    for c in fetch[5:]:
        c.wait()
    for k in range(4):
        lanes = pl.ds(128 * k, 128)
        dens[:, lanes] = density_of([pops_v[q, :, lanes].astype(f32) for q in range(19)])

    def first(i, carry):
        lanes = pl.ds(pl.multiple_of(i * 128, 128), 128)
        g = [pops_v[q, :, lanes].astype(f32) for q in range(19)]
        made = collide(g, solid_v[:, lanes] > 0, None, range(19))
        for q in range(19):
            post[q, i, 0:16, :] = made[q]
        return carry

    def collide_first():
        lax.fori_loop(0, 4, first, 0)
        for q in range(19):
            rel[ZPLACE[q]] = lane_roll(wide(post, q, pl.ds(0, 16)), VELOCITIES[q][2]).astype(bf16)
        rel[ZPLACE[FLAG]] = jnp.where(solid_v[...] > 0, 1.0, 0.0).astype(bf16)

    @pl.when(server)
    def _():
        collide_first()

    pl.semaphore_wait(barrier, len(NEAR) + jnp.where(server, 63, 64))
    density_copy = rows_copy(dens, mdens, pair_send.at[0], pair_recv.at[0], partner)
    source_copy = rows_copy(msrc, gsrc, pair_send.at[1], pair_recv.at[1], partner)

    pl.when(jnp.logical_not(server))(density_copy.start)
    send_requests(ask, asked, ask_send, ask_recv, z, d)
    pl.when(jnp.logical_not(server))(collide_first)

    def within(dz):
        return {-1: gz > 0, 0: None, 1: gz < 127}[dz]

    def if_within(dz, act):
        if dz:
            pl.when(within(dz))(act)
        else:
            act()

    zcopies = [
        remote(rel.at[pl.ds(0, 15)], below, zsend.at[0], zrecv.at[0], *beside(1, 0)),
        remote(rel.at[pl.ds(5, 15)], above, zsend.at[1], zrecv.at[1], *beside(-1, 0)),
    ]
    if_within(1, zcopies[0].start)
    if_within(-1, zcopies[1].start)

    def answer_half(half):
        wait_bytes(asked.at[half], ask_recv.at[half])
        reply, slots = look_up(asked[half, :, 0:8], lookup_field(dens[...], mdens[...]))
        tell[half, :, 0:8] = reply
        return slots

    @pl.when(server)
    def _():
        density_copy.wait_recv()
        slots = answer_half(0)
        send_answers(tell, told, tell_send, tell_recv, 0, z, d)
        total[...] = scatter(*slots)

    if_within(-1, zcopies[0].wait_recv)
    if_within(1, zcopies[1].wait_recv)
    has_below, has_above = gz > 0, gz < 127
    for q in range(20):
        cz, i = VELOCITIES[q][0], ZPLACE[q]
        mine = rel[i].astype(f32)
        if cz >= 0:
            under = jnp.where(has_below, below[i].astype(f32), 0.0)
        if cz <= 0:
            over = jnp.where(has_above, above[i - 5].astype(f32), 0.0)
        if cz == 1:
            rows = [under, mine]
        elif cz == -1:
            rows = [mine, over]
        else:
            rows = [under[8:16], mine, over[0:8]]
        put(work, q, pl.ds(0, 32), jnp.concatenate(rows, axis=0))

    def column(q, x):
        return wide(work, q, pl.ds(x, 4, stride=8))

    def edge_tile(q):
        cx = VELOCITIES[q][1]
        first_x, then_x = {0: (7, 0), 1: (7, 6), -1: (0, 1)}[cx]
        return jnp.concatenate([column(q, first_x), column(q, then_x)], axis=0)

    for b in range(11):
        edge[b] = jnp.concatenate([edge_tile(XTILES[2 * b]), edge_tile(XTILES[2 * b + 1])], axis=0).astype(bf16)
    to_right, to_left = beside(0, 1), beside(0, -1)
    xcopies = [
        remote(edge.at[pl.ds(0, 8)], left, xsend.at[0], xrecv.at[0], *to_right),
        remote(edge.at[pl.ds(3, 8)], right, xsend.at[1], xrecv.at[1], *to_left),
    ]
    for c in xcopies:
        c.start()

    @pl.when(server)
    def _():
        both = total[...] + scatter(*answer_half(1))
        msrc[...] = block_of(both, 1).astype(bf16)
        source_copy.start()
        src[...] = jnp.where(solid_v[...] > 0, 0.0, block_of(both, 0)).astype(bf16)

    @pl.when(jnp.logical_not(server))
    def _():
        source_copy.wait_recv()
        src[...] = jnp.where(solid_v[...] > 0, 0.0, gsrc[...].astype(f32)).astype(bf16)

    ncopies = []
    for i, (dz, dx) in enumerate(NEAR):
        ncopies.append(remote(src, near.at[7 - i], nsend.at[i], nrecv.at[7 - i], *beside(dz, dx)))
        if_within(dz, ncopies[-1].start)

    @pl.when(server)
    def _():
        send_answers(tell, told, tell_send, tell_recv, 1, z, d)

    for c in xcopies:
        c.wait_recv()
    has_left, has_right = col > 0, col < 3
    row8 = iota((8, 512), 0)

    def tile(ref, shift, q, there):
        k = XPLACE[q] - shift
        both = jnp.where(there, ref[k // 2].astype(f32), 0.0)
        return both[8 * (k % 2) : 8 * (k % 2) + 8]

    for q in range(20):
        cx = VELOCITIES[q][1]
        if cx == 0:
            put(work, q, pl.ds(32, 8), jnp.where(row8 < 4, tile(left, 0, q, has_left), tile(right, 6, q, has_right)))
        else:
            ends = tile(left, 0, q, has_left) if cx == 1 else tile(right, 6, q, has_right)
            k = XPLACE[q]
            mine = edge[k // 2].astype(f32)[8 * (k % 2) : 8 * (k % 2) + 8]
            merged = jnp.where(row8 < 4, mine, ends)
            put(work, q, pl.ds(32, 8), row_roll(merged, 4) if cx == 1 else merged)
            put(work, q, pl.ds(0, 32), row_roll(wide(work, q, pl.ds(0, 32)), cx))
            put(work, q, pl.ds(0 if cx == 1 else 7, 4, stride=8), ends[0:4])

    for i, (dz, dx) in enumerate(NEAR):
        if_within(dz, ncopies[7 - i].wait_recv)
    for a in (-1, 0, 1):
        for b in (-1, 0, 1):
            there = True
            if (a, b) == (0, 0):
                block = src[...].astype(f32)
            else:
                block = near[NEAR.index((a, b))].astype(f32)
                if a:
                    there = has_below if a < 0 else has_above
                if b:
                    sideways = has_left if b < 0 else has_right
                    there = jnp.logical_and(there, sideways) if a else sideways
                block = jnp.where(there, block, 0.0)
            for k in (0, 1):
                plane = block[8 * k : 8 * k + 8]
                at = 16 * (2 * (a + 1) + k)
                for cy in (-1, 0, 1):
                    moved = lane_roll(plane, cy)
                    if b == 0:
                        put(spread, cy + 1, pl.ds(at + 2, 8), moved)
                    elif b < 0:
                        put(spread, cy + 1, pl.ds(at, 2), moved[6:8])
                    else:
                        put(spread, cy + 1, pl.ds(at + 10, 2), moved[0:2])
    for q in range(20):
        cz, cx, cy = VELOCITIES[q]
        rows = [pl.ds(16 * (p + 1 - cz) + 2 - cx, 8) for p in range(4)]
        rows += [pl.ds(16 * (1 - cz) + k - cx, 4, stride=16) for k in (1, 10)]
        for c in range(4):
            added = jnp.concatenate([spread[cy + 1, c, r, :] for r in rows], axis=0)
            if q == FLAG:
                post[FLAG, c] = added
            else:
                work[q, c] = (work[q, c] + added).astype(bf16).astype(f32)

    row = iota((8, 128), 0)
    plane_in = jnp.logical_and(
        jnp.logical_or((row & 3) != 0, has_below), jnp.logical_or((row & 3) != 3, has_above)
    )
    side_in = jnp.logical_or(jnp.logical_and(row < 4, has_left), jnp.logical_and(row >= 4, has_right))
    edge_in = jnp.logical_and(plane_in, side_in)
    jobs = [(8, range(19), None), (16, range(19), None), (0, UP, has_below), (24, DOWN, has_above), (32, XUP + XDOWN, edge_in)]

    def second(i, carry):
        for r, wanted, inside in jobs:
            rows = pl.ds(r, 8)
            g = [work[q, i, rows, :] for q in range(19)]
            made = collide(g, work[FLAG, i, rows, :] > 0.5, post[FLAG, i, rows, :], wanted)
            for q in wanted:
                post[q, i, rows, :] = made[q] if inside is None else jnp.where(inside, made[q], 0.0)
        return carry

    lax.fori_loop(0, 4, second, 0)
    for q in range(19):
        cz, cx, cy = VELOCITIES[q]
        r = 8 * (1 - cz)
        moved = wide(post, q, pl.ds(r, 16))
        if cx:
            moved = row_roll(moved, cx)
            rim = 32 + (1 - cz) if cx == 1 else 36 + (1 - cz)
            for k in (0, 1):
                at = 8 * k + (0 if cx == 1 else 7)
                moved = jnp.where(iota((16, 512), 0) == at, wide(post, q, pl.ds(rim + k, 1)), moved)
        out[q] = lane_roll(moved, cy).astype(bf16)

    wait_bytes(told, tell_recv)
    line = coef * read_reply(told[:, 0:8], named_ref[...], rank)
    for k in (0, 1):
        row = line[:, 128 * k : 128 * k + 128]
        flux[k : k + 1, :] = row
        ice_left[k : k + 1, :] = ice_v[k : k + 1, :] - row
    if_within(1, zcopies[0].wait_send)
    if_within(-1, zcopies[1].wait_send)
    for c in xcopies:
        c.wait_send()
    for i, (dz, dx) in enumerate(NEAR):
        if_within(dz, ncopies[i].wait_send)

    @pl.when(server)
    def _():
        wait_bytes(ask.at[pl.ds(0, 126)], ask_send)
        wait_bytes(tell.at[0, pl.ds(0, 126)], tell_send)
        wait_bytes(tell.at[1], tell_send)
        source_copy.wait_send()

    @pl.when(jnp.logical_not(server))
    def _():
        wait_bytes(ask, ask_send)
        density_copy.wait_send()


def hand_over(a, b, c, x, y, z, sems):
    copies = [pltpu.make_async_copy(s, t, sems.at[i]) for i, (s, t) in enumerate([(a, x), (b, y), (c, z)])]
    for one in copies:
        one.start()
    for one in copies:
        one.wait()


def body(populations, solid, radius, rate, ice_mass, owner, voxel):
    vm = pl.BlockSpec(memory_space=pltpu.VMEM)
    hbm = pl.BlockSpec(memory_space=pltpu.HBM)
    sem = pltpu.SemaphoreType.DMA
    pair = jax.ShapeDtypeStruct((2, 128), f32)
    small = [pltpu.VMEM((2, 128), jnp.int32)] * 2 + [pltpu.VMEM((2, 128), f32)] * 3
    operands = [x.reshape(2, 128) for x in (owner, voxel, radius, rate, ice_mass)]
    operands += [solid.reshape(16, 512), populations.reshape(19, 16, 512)]
    moved = pl.pallas_call(
        step_pair,
        out_shape=(jax.ShapeDtypeStruct((19, 16, 512), bf16), pair, pair),
        in_specs=[hbm] * 7,
        out_specs=(vm,) * 3,
        scratch_shapes=small
        + [pltpu.VMEM((16, 512), jnp.int32), pltpu.VMEM((19, 16, 512), bf16)]
        + [pltpu.VMEM((128, 128), f32), pltpu.VMEM((2, 128, 128), f32)] * 2
        + [pltpu.VMEM((20, 16, 512), bf16)]
        + [pltpu.VMEM((15, 16, 512), bf16)] * 2
        + [pltpu.VMEM((11, 16, 512), bf16)]
        + [pltpu.VMEM((8, 16, 512), bf16)] * 2
        + [pltpu.VMEM((16, 512), bf16), pltpu.VMEM((8, 16, 512), bf16)]
        + [pltpu.VMEM((3, 4, 96, 128), f32)]
        + [pltpu.VMEM((20, 4, 40, 128), f32)] * 2
        + [pltpu.VMEM((16, 512), f32), pltpu.VMEM((128, 256), bf16), pltpu.VMEM((16, 512), f32), pltpu.VMEM((128, 128), f32)]
        + [pltpu.VMEM((16, 512), bf16)] * 2
        + [sem((7,)), sem, sem((2,)), sem, sem]
        + [sem((2,))] * 6
        + [sem((8,))] * 2,
        name="two_steps",
        compiler_params=pltpu.CompilerParams(collective_id=0, has_side_effects=True, vmem_limit_bytes=48 * 2**20),
    )(*[pltpu.with_memory_space_constraint(x, pltpu.HBM) for x in operands])
    state, flux, ice_left = pl.pallas_call(
        hand_over,
        out_shape=(jax.ShapeDtypeStruct((19, 16, 512), bf16), pair, pair),
        in_specs=[vm] * 3,
        out_specs=(hbm,) * 3,
        scratch_shapes=[sem((3,))],
        name="hand_over",
        compiler_params=pltpu.CompilerParams(vmem_limit_bytes=4 * 2**20),
    )(*[pltpu.with_memory_space_constraint(x, pltpu.VMEM) for x in moved])
    return (state.reshape(populations.shape), flux.reshape(-1), ice_left.reshape(-1))


def solution(mesh):
    return jax.shard_map(
        body,
        mesh=mesh,
        in_specs=(
            P(None, "gz", "col", None),
            P("gz", "col", None),
            P(("gz", "col")),
            P(("gz", "col")),
            P(("gz", "col")),
            P(("gz", "col"), None),
            P(("gz", "col")),
        ),
        out_specs=(P(None, "gz", "col", None), P(("gz", "col")), P(("gz", "col"))),
        check_vma=False,
    )
```

```python
import jax
import jax.numpy as jnp
from jax import lax
from jax.experimental import pallas as pl
from jax.experimental.pallas import tpu as pltpu
from jax.sharding import PartitionSpec as P

MESH = pl.DeviceIdType.MESH
HIGHEST = lax.Precision.HIGHEST
f32 = jnp.float32
bf16 = jnp.bfloat16


def hops(pair):
    o, e = pair
    return min(o, 8 - o) + min(e, 16 - e) / 2


PEERS = sorted([(o, e) for o in range(8) for e in range(16) if (o, e) != (0, 0)], key=lambda p: -hops(p))

TURNS = sorted(range(16), key=lambda e: -min(e, 16 - e))


def peer(z, d, o, e):
    return lax.rem(z + o, 8) * 16 + lax.rem(d + e, 16)


def greet_group(sem, z, d):
    for o, e in PEERS:
        pl.semaphore_signal(sem, inc=1, device_id={"gz": peer(z, d, o, e)}, device_id_type=MESH)


def rows_of(place):
    return pl.ds(pl.multiple_of(2 * place, 2), 2)


def rows_copy(src, dst, send, recv, gz):
    return pltpu.make_async_remote_copy(
        src_ref=src, dst_ref=dst, send_sem=send, recv_sem=recv, device_id={"gz": gz}, device_id_type=MESH
    )


def wait_bytes(rows, sem):
    pltpu.make_async_copy(rows, rows, sem).wait()


def send_requests(ask, asked, send, recv, z, d):
    half, level = z // 4, lax.rem(z, 4)
    for e in TURNS:
        for there in range(4):
            src = ask.at[rows_of(there * 16 + e)]
            dst = asked.at[half, rows_of(level * 16 + e)]
            copy = rows_copy(src, dst, send, recv.at[half], there * 16 + lax.rem(d + e, 16))
            if e:
                copy.start()
            else:
                pl.when(z != there)(copy.start)
                pl.when(z == there)(pltpu.make_async_copy(src, dst, recv.at[half]).start)


def send_answers(tell, told, send, recv, half, z, d):
    for e in TURNS:
        for level in range(4):
            src = tell.at[half, rows_of(level * 16 + e)]
            dst = told.at[rows_of(z * 16 + e)]
            to = 4 * half + level
            copy = rows_copy(src, dst, send, recv, to * 16 + lax.rem(d + 16 - e, 16))
            if e or half:
                copy.start()
            else:
                pl.when(z != to)(copy.start)
                pl.when(z == to)(pltpu.make_async_copy(src, dst, recv).start)


def iota(shape, dim):
    return lax.broadcasted_iota(jnp.int32, shape, dim)


def flat_row(ref):
    return jnp.concatenate([ref[0:1, :], ref[1:2, :]], axis=1)


def dot_t(a, b):
    return lax.dot_general(a, b, (((1,), (1,)), ((), ())), precision=HIGHEST, preferred_element_type=f32)


def dot(a, b):
    return jnp.dot(a, b, precision=HIGHEST, preferred_element_type=f32)


def request_table(own_ref, vox_ref, rad_ref, rate_ref, d):
    own, vox = flat_row(own_ref), flat_row(vox_ref)
    rad, rate = flat_row(rad_ref), flat_row(rate_ref)
    coef = rate * rad * rad
    level, upper = own >> 4, own >> 6
    rel = 2 * (jnp.where(upper > 0, 7 - level, level) * 16 + (((own & 15) - d) & 15)) + upper
    named = (iota((128, 256), 0) == rel).astype(f32)
    earlier = (iota((256, 256), 0) < iota((256, 256), 1)).astype(bf16)
    before = jnp.dot(named.astype(bf16), earlier, preferred_element_type=f32)
    rank = jnp.sum(before * named, axis=0, keepdims=True).astype(jnp.int32)
    lane = iota((128, 256), 0)
    value = jnp.where(lane < 4, coef, jnp.where(lane < 8, vox.astype(f32), 0.0))
    value = jnp.where((lane & 3) == rank, value, 0.0)
    return dot_t(named, value), named, rank, coef


def parts(x):
    high = x.astype(bf16)
    rest = x - high.astype(f32)
    middle = rest.astype(bf16)
    return [high, middle, (rest - middle.astype(f32)).astype(bf16)]


def lookup_field(own, other):
    field = jnp.concatenate([x[:, c * 128 : (c + 1) * 128] for x in (own, other) for c in range(4)], axis=0)
    return jnp.concatenate(parts(jnp.transpose(field)), axis=1)


def look_up(table, field):
    rows = jnp.transpose(table)
    coef = jnp.concatenate([rows[k : k + 1, :] for k in range(4)], axis=1)
    code = jnp.concatenate([rows[k : k + 1, :] for k in range(4, 8)], axis=1).astype(jnp.int32)
    hi = (iota((1, 512), 1) & 1) * 64 + ((code >> 7) & 3) * 16 + (code >> 9)
    at_lo = iota((128, 512), 0) == (code & 127)
    at_hi = ((iota((384, 512), 0) & 127) == hi).astype(f32).astype(bf16)
    picked = jnp.dot(field, at_hi, preferred_element_type=f32)
    answer = 2.0 - jnp.sum(jnp.where(at_lo, picked, 0.0), axis=0, keepdims=True)
    reply = jnp.concatenate([answer[:, k * 128 : (k + 1) * 128] for k in range(4)] + [jnp.zeros((4, 128), f32)], axis=0)
    return jnp.transpose(reply), (coef * answer, at_lo, at_hi[0:128])


def scatter(flux, at_lo, at_hi):
    spread = jnp.concatenate(parts(jnp.where(at_lo, 0.5 * flux, 0.0)), axis=1)
    where = jnp.concatenate([at_hi] * 3, axis=1)
    return lax.dot_general(where, spread, (((1,), (1,)), ((), ())), preferred_element_type=f32)


def block_of(total, k):
    return jnp.concatenate([total[64 * k + 16 * c : 64 * k + 16 * c + 16, :] for c in range(4)], axis=1)


def read_reply(reply, named, rank):
    rows = jnp.transpose(reply)
    got = jnp.dot(jnp.concatenate(parts(rows), axis=0), named, preferred_element_type=f32)
    got = got[0:8] + got[8:16] + got[16:24]
    return jnp.sum(jnp.where(iota((8, 256), 0) == rank, got, 0.0), axis=0, keepdims=True)


VELOCITIES = [
    (0, 0, 0),
    (1, 0, 0),
    (-1, 0, 0),
    (0, 1, 0),
    (0, -1, 0),
    (0, 0, 1),
    (0, 0, -1),
    (1, 1, 0),
    (-1, -1, 0),
    (1, -1, 0),
    (-1, 1, 0),
    (1, 0, 1),
    (-1, 0, -1),
    (1, 0, -1),
    (-1, 0, 1),
    (0, 1, 1),
    (0, -1, -1),
    (0, 1, -1),
    (0, -1, 1),
    (0, 0, 0),
]
FLAG = 19
UP = [q for q in range(19) if VELOCITIES[q][0] == 1]
FLAT = [q for q in range(20) if VELOCITIES[q][0] == 0]
DOWN = [q for q in range(19) if VELOCITIES[q][0] == -1]
XUP = [q for q in range(19) if VELOCITIES[q][1] == 1]
XFLAT = [q for q in range(20) if VELOCITIES[q][1] == 0]
XDOWN = [q for q in range(19) if VELOCITIES[q][1] == -1]
NEAR = [(a, b) for a in (-1, 0, 1) for b in (-1, 0, 1) if (a, b) != (0, 0)]
ASIDE = [(a, b) for a, b in NEAR if b != 0]


def dotc(c, v):
    total = None
    for k, x in zip(c, v):
        if k:
            total = (x if k > 0 else -x) if total is None else (total + x if k > 0 else total - x)
    return total


def total_of(terms):
    out = terms[0]
    for t in terms[1:]:
        out = out + t
    return out


def density_of(g):
    near = total_of([g[q] for q in range(1, 7)])
    far = total_of([g[q] for q in range(7, 19)])
    return g[0] * (1.0 / 3.0) + near * (1.0 / 18.0) + far * (1.0 / 36.0)


def collide(g, solid, source, wanted):
    diff = {q: g[q] - g[q + 1] for q in range(1, 19, 2)}
    rho = density_of(g)
    j = []
    for axis in range(3):
        far = None
        for q in range(7, 19, 2):
            k = VELOCITIES[q][axis]
            if k:
                far = diff[q] if far is None else (far + diff[q] if k > 0 else far - diff[q])
        j.append(diff[1 + 2 * axis] * (4.8 / 18.0) + far * (4.8 / 36.0))
    scale = (1.5 / 4.8) / rho
    u = [x * scale for x in j]
    own = [x * y for x, y in zip(j, u)]
    base = 1.6 * rho - (own[0] + own[1] + own[2]) * (1.0 / 3.0)
    if source is not None:
        base = base + source
    out = {}
    if 0 in wanted:
        out[0] = jnp.where(solid, g[0], base - 0.6 * g[0])
    for q in range(1, 19, 2):
        if q not in wanted and q + 1 not in wanted:
            continue
        odd = dotc(VELOCITIES[q], j)
        even = base + (own[q // 2] if q < 7 else odd * dotc(VELOCITIES[q], u))
        if q in wanted:
            out[q] = jnp.where(solid, g[q + 1], even + odd - 0.6 * g[q])
        if q + 1 in wanted:
            out[q + 1] = jnp.where(solid, g[q], even - odd - 0.6 * g[q + 1])
    return out


def wide(ref, q, rows):
    return jnp.concatenate([ref[q, c, rows, :] for c in range(4)], axis=1)


def put(ref, q, rows, value):
    for c in range(4):
        ref[q, c, rows, :] = value[:, 128 * c : 128 * c + 128]


def lane_roll(x, cy):
    return x if cy == 0 else pltpu.roll(x, cy % 512, 1)


def row_roll(x, k):
    return pltpu.roll(x, k % x.shape[0], 0)


def remote(src, dst, send, recv, gz, col):
    return pltpu.make_async_remote_copy(
        src_ref=src, dst_ref=dst, send_sem=send, recv_sem=recv, device_id={"gz": gz, "col": col}, device_id_type=MESH
    )


def step_pair(own, vox, rad, rate, ice, solid, pops, out, flux, ice_left, *scratch):
    (own_v, vox_v, rad_v, rate_v, ice_v, solid_v, pops_v, ask, asked, told, tell, rel, below, above, edge, left, right) = scratch[:17]
    (src, near, spread, work, post, dens, named_ref, mdens, total, msrc, gsrc) = scratch[17:28]
    (loads, ask_send, ask_recv, tell_send, tell_recv, pair_send, pair_recv, zsend, zrecv, xsend, xrecv, nsend, nrecv) = scratch[28:]
    gz, col = lax.axis_index("gz"), lax.axis_index("col")
    z, d = gz // 16, lax.rem(gz, 16)
    barrier = pltpu.get_barrier_semaphore()

    fetch = [
        pltpu.make_async_copy(a, b, loads.at[i])
        for i, (a, b) in enumerate(
            [(own, own_v), (vox, vox_v), (rad, rad_v), (rate, rate_v), (ice, ice_v), (solid, solid_v), (pops, pops_v)]
        )
    ]
    for c in fetch:
        c.start()
    server, partner = z < 4, (7 - z) * 16 + d

    def beside(dz, dx):
        return lax.rem(gz + dz + 128, 128), lax.rem(col + dx + 4, 4)

    for dz, dx in NEAR:
        g, c = beside(dz, dx)
        pl.semaphore_signal(barrier, inc=1, device_id={"gz": g, "col": c}, device_id_type=MESH)

    @pl.when(server)
    def _():
        greet_group(barrier, z, d)

    for c in fetch[:5]:
        c.wait()
    table, named, rank, coef = request_table(own_v, vox_v, rad_v, rate_v, d)
    ask[...] = table
    named_ref[...] = named.astype(bf16)
    for c in fetch[5:]:
        c.wait()
    for k in range(4):
        lanes = pl.ds(128 * k, 128)
        dens[:, lanes] = density_of([pops_v[q, :, lanes].astype(f32) for q in range(19)])

    def first(i, carry):
        lanes = pl.ds(pl.multiple_of(i * 128, 128), 128)
        g = [pops_v[q, :, lanes].astype(f32) for q in range(19)]
        made = collide(g, solid_v[:, lanes] > 0, None, range(19))
        for q in range(19):
            post[q, i, 0:16, :] = made[q]
        return carry

    def collide_first():
        lax.fori_loop(0, 4, first, 0)
        for q in range(19):
            if VELOCITIES[q][0]:
                at = UP.index(q) if q in UP else 15 + DOWN.index(q)
                rel[at] = lane_roll(wide(post, q, pl.ds(0, 16)), VELOCITIES[q][2]).astype(bf16)
        for k in range(5):
            two = []
            for q in FLAT[2 * k : 2 * k + 2]:
                if q == FLAG:
                    two.append(jnp.where(solid_v[...] > 0, 1.0, 0.0))
                else:
                    two.append(lane_roll(wide(post, q, pl.ds(0, 16)), VELOCITIES[q][2]))
            rel[5 + k] = jnp.concatenate([x[8:16] for x in two], axis=0).astype(bf16)
            rel[10 + k] = jnp.concatenate([x[0:8] for x in two], axis=0).astype(bf16)

    @pl.when(server)
    def _():
        collide_first()

    pl.semaphore_wait(barrier, len(NEAR) + jnp.where(server, 63, 64))
    density_copy = rows_copy(dens, mdens, pair_send.at[0], pair_recv.at[0], partner)
    source_copy = rows_copy(msrc, gsrc, pair_send.at[1], pair_recv.at[1], partner)

    pl.when(jnp.logical_not(server))(density_copy.start)
    send_requests(ask, asked, ask_send, ask_recv, z, d)
    pl.when(jnp.logical_not(server))(collide_first)

    def within(dz):
        return {-1: gz > 0, 0: None, 1: gz < 127}[dz]

    def if_within(dz, act):
        if dz:
            pl.when(within(dz))(act)
        else:
            act()

    zcopies = [
        remote(rel.at[pl.ds(0, 10)], below, zsend.at[0], zrecv.at[0], *beside(1, 0)),
        remote(rel.at[pl.ds(10, 10)], above, zsend.at[1], zrecv.at[1], *beside(-1, 0)),
    ]
    if_within(1, zcopies[0].start)
    if_within(-1, zcopies[1].start)

    def answer_half(half):
        wait_bytes(asked.at[half], ask_recv.at[half])
        reply, slots = look_up(asked[half, :, 0:8], lookup_field(dens[...], mdens[...]))
        tell[half, :, 0:8] = reply
        return slots

    @pl.when(server)
    def _():
        density_copy.wait_recv()
        slots = answer_half(0)
        send_answers(tell, told, tell_send, tell_recv, 0, z, d)
        total[...] = scatter(*slots)

    if_within(-1, zcopies[0].wait_recv)
    if_within(1, zcopies[1].wait_recv)
    has_below, has_above = gz > 0, gz < 127
    for k in range(5):
        under, mine = jnp.where(has_below, below[k].astype(f32), 0.0), rel[k].astype(f32)
        put(work, UP[k], pl.ds(0, 32), jnp.concatenate([under, mine], axis=0))
        mine, over = rel[15 + k].astype(f32), jnp.where(has_above, above[5 + k].astype(f32), 0.0)
        put(work, DOWN[k], pl.ds(0, 32), jnp.concatenate([mine, over], axis=0))
        under, over = jnp.where(has_below, below[5 + k].astype(f32), 0.0), jnp.where(has_above, above[k].astype(f32), 0.0)
        upper, lower = rel[5 + k].astype(f32), rel[10 + k].astype(f32)
        for half in (0, 1):
            planes = [x[8 * half : 8 * half + 8] for x in (under, lower, upper, over)]
            put(work, FLAT[2 * k + half], pl.ds(0, 32), jnp.concatenate(planes, axis=0))

    def column(q, x):
        return wide(work, q, pl.ds(x, 4, stride=8))

    def tile_of(first_tile, then_tile):
        return jnp.concatenate([column(*first_tile), column(*then_tile)], axis=0)

    flats = [(XFLAT[2 * k], XFLAT[2 * k + 1]) for k in range(5)]
    tiles = [((q, 7), (q, 6)) for q in XUP] + [((a, 7), (b, 7)) for a, b in flats]
    tiles += [((a, 0), (b, 0)) for a, b in flats] + [((q, 0), (q, 1)) for q in XDOWN]
    for b in range(10):
        edge[b] = jnp.concatenate([tile_of(*tiles[2 * b]), tile_of(*tiles[2 * b + 1])], axis=0).astype(bf16)
    to_right, to_left = beside(0, 1), beside(0, -1)
    xcopies = [
        remote(edge.at[pl.ds(0, 5)], left, xsend.at[0], xrecv.at[0], *to_right),
        remote(edge.at[pl.ds(5, 5)], right, xsend.at[1], xrecv.at[1], *to_left),
    ]
    for c in xcopies:
        c.start()

    @pl.when(server)
    def _():
        both = total[...] + scatter(*answer_half(1))
        msrc[...] = block_of(both, 1).astype(bf16)
        source_copy.start()
        src[...] = jnp.where(solid_v[...] > 0, 0.0, block_of(both, 0)).astype(bf16)

    @pl.when(jnp.logical_not(server))
    def _():
        source_copy.wait_recv()
        src[...] = jnp.where(solid_v[...] > 0, 0.0, gsrc[...].astype(f32)).astype(bf16)

    ncopies = []
    for i, (dz, dx) in enumerate(NEAR):
        ncopies.append(remote(src, near.at[7 - i], nsend.at[i], nrecv.at[7 - i], *beside(dz, dx)))
        if_within(dz, ncopies[-1].start)

    @pl.when(server)
    def _():
        send_answers(tell, told, tell_send, tell_recv, 1, z, d)

    for c in xcopies:
        c.wait_recv()
    has_left, has_right = col > 0, col < 3
    row8 = iota((8, 512), 0)

    def tile(ref, k, there=None):
        both = ref[k // 2].astype(f32)[8 * (k % 2) : 8 * (k % 2) + 8]
        return both if there is None else jnp.where(there, both, 0.0)

    for k in range(5):
        from_left, from_right = tile(left, 5 + k, has_left), tile(right, k, has_right)
        put(work, flats[k][0], pl.ds(32, 8), jnp.where(row8 < 4, from_left, row_roll(from_right, 4)))
        put(work, flats[k][1], pl.ds(32, 8), jnp.where(row8 < 4, row_roll(from_left, 4), from_right))
        q, ends = XUP[k], tile(left, k, has_left)
        put(work, q, pl.ds(32, 8), row_roll(jnp.where(row8 < 4, tile(edge, k), ends), 4))
        put(work, q, pl.ds(0, 32), row_roll(wide(work, q, pl.ds(0, 32)), 1))
        put(work, q, pl.ds(0, 4, stride=8), ends[0:4])
        q, ends = XDOWN[k], tile(right, 5 + k, has_right)
        put(work, q, pl.ds(32, 8), jnp.where(row8 < 4, tile(edge, 15 + k), ends))
        put(work, q, pl.ds(0, 32), row_roll(wide(work, q, pl.ds(0, 32)), -1))
        put(work, q, pl.ds(7, 4, stride=8), ends[0:4])

    for i, (dz, dx) in enumerate(NEAR):
        if_within(dz, ncopies[7 - i].wait_recv)
    for a in (-1, 0, 1):
        for b in (-1, 0, 1):
            there = True
            if (a, b) == (0, 0):
                block = src[...].astype(f32)
            else:
                block = near[NEAR.index((a, b))].astype(f32)
                if a:
                    there = has_below if a < 0 else has_above
                if b:
                    sideways = has_left if b < 0 else has_right
                    there = jnp.logical_and(there, sideways) if a else sideways
                block = jnp.where(there, block, 0.0)
            for k in (0, 1):
                plane = block[8 * k : 8 * k + 8]
                at = 16 * (2 * (a + 1) + k)
                for cy in (-1, 0, 1):
                    moved = lane_roll(plane, cy)
                    if b == 0:
                        put(spread, cy + 1, pl.ds(at + 2, 8), moved)
                    elif b < 0:
                        put(spread, cy + 1, pl.ds(at, 2), moved[6:8])
                    else:
                        put(spread, cy + 1, pl.ds(at + 10, 2), moved[0:2])
    for q in range(20):
        cz, cx, cy = VELOCITIES[q]
        rows = [pl.ds(16 * (p + 1 - cz) + 2 - cx, 8) for p in range(4)]
        rows += [pl.ds(16 * (1 - cz) + k - cx, 4, stride=16) for k in (1, 10)]
        for c in range(4):
            added = jnp.concatenate([spread[cy + 1, c, r, :] for r in rows], axis=0)
            if q == FLAG:
                post[FLAG, c] = added
            else:
                work[q, c] = (work[q, c] + added).astype(bf16).astype(f32)

    row = iota((8, 128), 0)
    plane_in = jnp.logical_and(
        jnp.logical_or((row & 3) != 0, has_below), jnp.logical_or((row & 3) != 3, has_above)
    )
    side_in = jnp.logical_or(jnp.logical_and(row < 4, has_left), jnp.logical_and(row >= 4, has_right))
    edge_in = jnp.logical_and(plane_in, side_in)
    jobs = [(8, range(19), None), (16, range(19), None), (0, UP, has_below), (24, DOWN, has_above), (32, XUP + XDOWN, edge_in)]

    def second(i, carry):
        for r, wanted, inside in jobs:
            rows = pl.ds(r, 8)
            g = [work[q, i, rows, :] for q in range(19)]
            made = collide(g, work[FLAG, i, rows, :] > 0.5, post[FLAG, i, rows, :], wanted)
            for q in wanted:
                post[q, i, rows, :] = made[q] if inside is None else jnp.where(inside, made[q], 0.0)
        return carry

    lax.fori_loop(0, 4, second, 0)
    for q in range(19):
        cz, cx, cy = VELOCITIES[q]
        r = 8 * (1 - cz)
        moved = wide(post, q, pl.ds(r, 16))
        if cx:
            moved = row_roll(moved, cx)
            rim = 32 + (1 - cz) if cx == 1 else 36 + (1 - cz)
            for k in (0, 1):
                at = 8 * k + (0 if cx == 1 else 7)
                moved = jnp.where(iota((16, 512), 0) == at, wide(post, q, pl.ds(rim + k, 1)), moved)
        out[q] = lane_roll(moved, cy).astype(bf16)

    wait_bytes(told, tell_recv)
    line = coef * read_reply(told[:, 0:8], named_ref[...], rank)
    for k in (0, 1):
        row = line[:, 128 * k : 128 * k + 128]
        flux[k : k + 1, :] = row
        ice_left[k : k + 1, :] = ice_v[k : k + 1, :] - row
    if_within(1, zcopies[0].wait_send)
    if_within(-1, zcopies[1].wait_send)
    for c in xcopies:
        c.wait_send()
    for i, (dz, dx) in enumerate(NEAR):
        if_within(dz, ncopies[i].wait_send)

    @pl.when(server)
    def _():
        wait_bytes(ask.at[pl.ds(0, 126)], ask_send)
        wait_bytes(tell.at[0, pl.ds(0, 126)], tell_send)
        wait_bytes(tell.at[1], tell_send)
        source_copy.wait_send()

    @pl.when(jnp.logical_not(server))
    def _():
        wait_bytes(ask, ask_send)
        density_copy.wait_send()


def hand_over(a, b, c, x, y, z, sems):
    copies = [pltpu.make_async_copy(s, t, sems.at[i]) for i, (s, t) in enumerate([(a, x), (b, y), (c, z)])]
    for one in copies:
        one.start()
    for one in copies:
        one.wait()


def body(populations, solid, radius, rate, ice_mass, owner, voxel):
    vm = pl.BlockSpec(memory_space=pltpu.VMEM)
    hbm = pl.BlockSpec(memory_space=pltpu.HBM)
    sem = pltpu.SemaphoreType.DMA
    pair = jax.ShapeDtypeStruct((2, 128), f32)
    small = [pltpu.VMEM((2, 128), jnp.int32)] * 2 + [pltpu.VMEM((2, 128), f32)] * 3
    operands = [x.reshape(2, 128) for x in (owner, voxel, radius, rate, ice_mass)]
    operands += [solid.reshape(16, 512), populations.reshape(19, 16, 512)]
    moved = pl.pallas_call(
        step_pair,
        out_shape=(jax.ShapeDtypeStruct((19, 16, 512), bf16), pair, pair),
        in_specs=[hbm] * 7,
        out_specs=(vm,) * 3,
        scratch_shapes=small
        + [pltpu.VMEM((16, 512), jnp.int32), pltpu.VMEM((19, 16, 512), bf16)]
        + [pltpu.VMEM((128, 128), f32), pltpu.VMEM((2, 128, 128), f32)] * 2
        + [pltpu.VMEM((20, 16, 512), bf16)]
        + [pltpu.VMEM((10, 16, 512), bf16)] * 3
        + [pltpu.VMEM((5, 16, 512), bf16)] * 2
        + [pltpu.VMEM((16, 512), bf16), pltpu.VMEM((8, 16, 512), bf16)]
        + [pltpu.VMEM((3, 4, 96, 128), f32)]
        + [pltpu.VMEM((20, 4, 40, 128), f32)] * 2
        + [pltpu.VMEM((16, 512), f32), pltpu.VMEM((128, 256), bf16), pltpu.VMEM((16, 512), f32), pltpu.VMEM((128, 128), f32)]
        + [pltpu.VMEM((16, 512), bf16)] * 2
        + [sem((7,)), sem, sem((2,)), sem, sem]
        + [sem((2,))] * 6
        + [sem((8,))] * 2,
        name="two_steps",
        compiler_params=pltpu.CompilerParams(collective_id=0, has_side_effects=True, vmem_limit_bytes=48 * 2**20),
    )(*[pltpu.with_memory_space_constraint(x, pltpu.HBM) for x in operands])
    state, flux, ice_left = pl.pallas_call(
        hand_over,
        out_shape=(jax.ShapeDtypeStruct((19, 16, 512), bf16), pair, pair),
        in_specs=[vm] * 3,
        out_specs=(hbm,) * 3,
        scratch_shapes=[sem((3,))],
        name="hand_over",
        compiler_params=pltpu.CompilerParams(vmem_limit_bytes=4 * 2**20),
    )(*[pltpu.with_memory_space_constraint(x, pltpu.VMEM) for x in moved])
    return (state.reshape(populations.shape), flux.reshape(-1), ice_left.reshape(-1))


def solution(mesh):
    return jax.shard_map(
        body,
        mesh=mesh,
        in_specs=(
            P(None, "gz", "col", None),
            P("gz", "col", None),
            P(("gz", "col")),
            P(("gz", "col")),
            P(("gz", "col")),
            P(("gz", "col"), None),
            P(("gz", "col")),
        ),
        out_specs=(P(None, "gz", "col", None), P(("gz", "col")), P(("gz", "col"))),
        check_vma=False,
    )
```
